32 devices in a mesh: dp: 8 (over y, x, core), tensor: 4 (over z).
Axes of the slice: x: 2, y: 2, z: 4, core: 2. Of those that a mesh axis runs over, the one named last changes fastest.
Arguments:
- inputs: bfloat16 [16, 711, 768], P('dp'), may hold values from -6 to 6
- caption_lengths: int32 [16], P('dp'), may hold values from 8 to 512, as said below
- g_attn: float32 [768], replicated, may hold values from 0.25 to 1.75
- c_attn: float32 [768], replicated, may hold values from -2 to 2
- w_qkv: bfloat16 [3, 768, 768], P(None, 'tensor'), may hold values from -0.21875 to 0.21875
- b_qv: float32 [2, 768], P(None, 'tensor'), may hold values from -2 to 2
- w_out: bfloat16 [768, 768], P('tensor'), may hold values from -2 to 2
- b_out: float32 [768], replicated, may hold values from -2 to 2
- g_mlp: float32 [768], replicated, may hold values from 0.25 to 1.75
- c_mlp: float32 [768], replicated, may hold values from -2 to 2
- w_up: bfloat16 [768, 3072], P(None, 'tensor'), may hold values from -0.21875 to 0.21875
- b_up: float32 [3072], P('tensor'), may hold values from -2 to 2
- w_down: bfloat16 [3072, 768], P('tensor'), may hold values from -0.109375 to 0.109375
- b_down: float32 [768], replicated, may hold values from -2 to 2
- out_grad: bfloat16 [16, 711, 768], P('dp'), may hold values from -6 to 6
Outputs:
- outputs: bfloat16 [16, 711, 768], P('dp')
- input_grad: float32 [16, 711, 768], P('dp')
- grad_g_attn: float32 [768], replicated
- grad_c_attn: float32 [768], replicated
- grad_w_qkv: float32 [3, 768, 768], P(None, 'tensor')
- grad_b_qv: float32 [2, 768], P(None, 'tensor')
- grad_w_out: float32 [768, 768], P('tensor')
- grad_b_out: float32 [768], replicated
- grad_g_mlp: float32 [768], replicated
- grad_c_mlp: float32 [768], replicated
- grad_w_up: float32 [768, 3072], P(None, 'tensor')
- grad_b_up: float32 [3072], P('tensor')
- grad_w_down: float32 [3072, 768], P('tensor')
- grad_b_down: float32 [768], replicated
The draws below stay inside these ranges and needn't reach their ends.
Inputs may be any that keep to these rules, and one draw needn't show every extreme that they name: `caption_lengths`: rows from 199 + a sequence's caption length on are padding.
All inputs are finite; a program needn't handle non-finite values.
Results may differ from the reference program's by a relative error of at most 0.012.
The reference program's roundings to bfloat16 on the way count: a program that leaves them out, or rounds other values in their place, can miss the bound.
Values sent between devices are 32-bit elements; how exact they have to be, the bound alone decides.
No kernel may reach another device: no remote copies, remote signals or barrier semaphores. Data moves between devices by JAX's collectives and lax.ppermute only.
A program may use at most 128 MiB of HBM per device.

```python
import jax
import jax.numpy as jnp
from jax import lax

D = 768
HEADS = 12
HEAD_DIM = 64
FF = 3072
IMAGE_ROWS = 198
TEXT_SLOTS = 513
ROWS = 711
SEQ_DEV = 2
SEQS = 16


def draw_caption_lengths(key, part):
    key = jax.random.fold_in(key, 11)
    keys = jax.random.split(key, 3)
    longest = TEXT_SLOTS - 1
    draws = jax.random.randint(keys[0], (4, SEQS), 8, longest + 1)
    lengths = jnp.min(draws, axis=0)
    top_at = jax.random.randint(keys[1], (), 0, SEQS)
    short_at = (top_at + jax.random.randint(keys[2], (), 1, SEQS)) % SEQS
    index = jnp.arange(SEQS)
    lengths = jnp.where(index == top_at, longest, lengths)
    lengths = jnp.where(index == short_at, 8, lengths)
    return lengths.astype(jnp.int32)


def levels(own_key, shape, cuts, least, high):
    level = 1.0
    for axis_at, shards_of in cuts:
        steps = jax.random.uniform(jax.random.fold_in(jax.random.fold_in(own_key, 6), axis_at), (shards_of,), jnp.float32, least / len(cuts), high / len(cuts))
        level = level * jnp.repeat(jnp.exp(steps), shape[axis_at] // shards_of).reshape((-1,) + (1,) * (len(shape) - 1 - axis_at))
    return level


def gaussian(key, extent, scale, reach, cuts=(), dtype=jnp.bfloat16):
    array = scale * jax.random.normal(key, extent, jnp.float32)
    if cuts:
        array = array * levels(key, extent, cuts, -0.22, 0.18)
    return jnp.clip(array, -reach, reach).astype(dtype)


def setup_inputs(seed: int = 0) -> dict:
    arg_keys = jax.random.split(jax.random.key(seed), 16)
    return {
        "inputs": gaussian(arg_keys[0], (SEQS, ROWS, D), 1.0, 6.0, ((0, 8),)),
        "caption_lengths": draw_caption_lengths(jax.random.fold_in(arg_keys[15], 71), 0),
        "g_attn": jnp.clip(1.0 + 0.15 * jax.random.normal(arg_keys[2], (D,), jnp.float32), 0.25, 1.75),
        "c_attn": gaussian(arg_keys[3], (D,), 0.3, 2.0, (), jnp.float32),
        "w_qkv": gaussian(arg_keys[4], (3, D, D), D ** -0.5, 0.21875, ((1, 4),)),
        "b_qv": gaussian(arg_keys[5], (2, D), 0.3, 2.0, ((1, 4),), jnp.float32),
        "w_out": gaussian(arg_keys[6], (D, D), 8 ** -0.5, 2.0, ((0, 4),)),
        "b_out": gaussian(arg_keys[7], (D,), 0.3, 2.0, (), jnp.float32),
        "g_mlp": jnp.clip(1.0 + 0.15 * jax.random.normal(arg_keys[8], (D,), jnp.float32), 0.25, 1.75),
        "c_mlp": gaussian(arg_keys[9], (D,), 0.3, 2.0, (), jnp.float32),
        "w_up": gaussian(arg_keys[10], (D, FF), D ** -0.5, 0.21875, ((1, 4),)),
        "b_up": gaussian(arg_keys[11], (FF,), 0.3, 2.0, ((0, 4),), jnp.float32),
        "w_down": gaussian(arg_keys[12], (FF, D), FF ** -0.5, 0.109375, ((0, 4),)),
        "b_down": gaussian(arg_keys[13], (D,), 0.3, 2.0, (), jnp.float32),
        "out_grad": gaussian(arg_keys[14], (SEQS, ROWS, D), 1.0, 6.0, ((0, 8),)),
    }


EPS = 1e-06
HIGH = lax.Precision.HIGHEST

@jax.custom_vjp
def low(v):
    return lax.optimization_barrier(v.astype(jnp.bfloat16)).astype(jnp.float32)

@jax.custom_vjp
def low_back(v):
    return v

def low_keep(v):
    return (low(v), None)

def low_pass(kept, grad):
    return (grad,)

def back_keep(v):
    return (v, None)

def back_low(kept, grad):
    return (low(grad),)
low.defvjp(low_keep, low_pass)
low_back.defvjp(back_keep, back_low)

def layer_norm(values, gain_vec, shift_vec):
    average = lax.optimization_barrier(jnp.mean(values, axis=-1, keepdims=True))
    centered = values - average
    squares = lax.optimization_barrier(jnp.mean(centered * centered, axis=-1, keepdims=True))
    return centered * lax.rsqrt(squares + EPS) * gain_vec + shift_vec

def attend_item(item):
    query_rows, key_rows, value_rows, usable = item
    scores = jnp.einsum('qhd,khd->hqk', query_rows, key_rows, precision=HIGH) * HEAD_DIM ** (-0.5)
    scores = low_back(scores)
    scores = jnp.where(usable[None, None, :] > 0.5, scores, -1e+30)
    highest = lax.optimization_barrier(jnp.max(scores, axis=-1, keepdims=True))
    weights = jnp.exp(scores - highest)
    weights = weights / lax.optimization_barrier(jnp.sum(weights, axis=-1, keepdims=True))
    return jnp.einsum('hqk,khd->qhd', low(weights), value_rows, precision=HIGH)

def layer(residual, usable, g_attn, c_attn, w_qkv, b_qv, w_out, b_out, g_mlp, c_mlp, w_up, b_up, w_down, b_down):
    batch_seqs = residual.shape[0]
    normed_in = low(layer_norm(residual, g_attn, c_attn))
    projected = jnp.einsum('srd,ted->tsre', normed_in, w_qkv, precision=HIGH)
    query_rows = low(low_back(projected[0]) + b_qv[0])
    key_rows = low(low_back(projected[1]))
    value_rows = low(low_back(projected[2]) + b_qv[1])
    head_shape = (batch_seqs, ROWS, HEADS, HEAD_DIM)
    mixture = lax.map(jax.checkpoint(attend_item), (query_rows.reshape(head_shape), key_rows.reshape(head_shape), value_rows.reshape(head_shape), usable))
    mixture = low_back(low(mixture.reshape(batch_seqs, ROWS, D)))
    hidden = residual + low_back(jnp.einsum('sre,ed->srd', mixture, w_out, precision=HIGH)) + b_out
    normed_mid = low(layer_norm(hidden, g_mlp, c_mlp))
    up_proj = low_back(jnp.einsum('srd,df->srf', normed_mid, w_up, precision=HIGH)) + b_up
    activated = low(jax.nn.gelu(up_proj, approximate=False))
    down_proj = low_back(jnp.einsum('srf,fd->srd', activated, w_down, precision=HIGH)) + b_down
    return (hidden + down_proj) * usable[..., None]

def reference(inputs, caption_lengths, g_attn, c_attn, w_qkv, b_qv, w_out, b_out, g_mlp, c_mlp, w_up, b_up, w_down, b_down, out_grad):
    params = tuple((weight.astype(jnp.float32) for weight in (g_attn, c_attn, w_qkv, b_qv, w_out, b_out, g_mlp, c_mlp, w_up, b_up, w_down, b_down)))
    positions = lax.broadcasted_iota(jnp.int32, (SEQS, ROWS), 1)
    usable = (positions < IMAGE_ROWS + 1 + caption_lengths[:, None].astype(jnp.int32)).astype(jnp.float32)
    groups = SEQS // SEQ_DEV

    def run_group(totals, item):
        block_in, block_use, block_grad = item
        result, pull_back = jax.vjp(lambda flat_in, *weights: layer(flat_in, block_use, *weights), block_in.astype(jnp.float32), *params)
        grads = pull_back(block_grad.astype(jnp.float32))
        totals = tuple((total + grad for total, grad in zip(totals, grads[1:])))
        return (totals, (result.astype(jnp.bfloat16), grads[0]))
    starts = tuple((jnp.zeros(weight.shape, jnp.float32) for weight in params))
    totals, (output_rows, grad_rows) = lax.scan(run_group, starts, (inputs.reshape(groups, SEQ_DEV, ROWS, D), usable.reshape(groups, SEQ_DEV, ROWS), out_grad.reshape(groups, SEQ_DEV, ROWS, D)))
    return (output_rows.reshape(SEQS, ROWS, D), grad_rows.reshape(SEQS, ROWS, D), totals[0], totals[1], totals[2], totals[3], totals[4], totals[5], totals[6], totals[7], totals[8], totals[9], totals[10], totals[11])
```

```python
import math
from functools import partial

import jax
import jax.numpy as jnp
from jax import lax
from jax.experimental import pallas as pl
from jax.experimental.pallas import tpu as pltpu
from jax.sharding import PartitionSpec as P

HEAD_DIM = 64
IMAGE_ROWS = 198
EPS = 1e-06
LOG2E = math.log2(math.e)
SCALE = HEAD_DIM ** (-0.5)
ROW_TILE = 16
QUERY_BLOCK = 128
SLACK = 256
COST_SCALE = 0.02
VMEM_LIMIT = 48 * 1024 * 1024

NT = (((1,), (1,)), ((), ()))
TN = (((0,), (0,)), ((), ()))


def mm(a, b, dims=None):
    if dims is None:
        return jnp.dot(a, b, preferred_element_type=jnp.float32)
    return lax.dot_general(a, b, dims, preferred_element_type=jnp.float32)


def params():
    return pltpu.CompilerParams(vmem_limit_bytes=VMEM_LIMIT)


def cost(flops, moved, trans=0):
    scale = COST_SCALE
    return pl.CostEstimate(
        flops=int(flops * scale) + 1, bytes_accessed=int(moved * scale) + 1, transcendentals=int(trans * scale)
    )


def sds(shape, dtype):
    return jax.ShapeDtypeStruct(shape, dtype)


def after(value, *earlier):
    return lax.optimization_barrier((value,) + earlier)[0]


VMEM_WHOLE = pl.BlockSpec(memory_space=pltpu.VMEM)
SMEM_WHOLE = pl.BlockSpec(memory_space=pltpu.SMEM)


def norm_parts(values):
    average = jnp.mean(values, axis=-1, keepdims=True)
    centered = values - average
    squares = jnp.mean(centered * centered, axis=-1, keepdims=True)
    inverse = lax.rsqrt(squares + EPS)
    return centered * inverse, inverse


def norm_input_grad(grad_rows, unit_rows, inverse, gain):
    scaled = grad_rows * gain
    first = jnp.mean(scaled, axis=-1, keepdims=True)
    second = jnp.mean(scaled * unit_rows, axis=-1, keepdims=True)
    return inverse * (scaled - first - unit_rows * second)


def column_sums(*arrays):
    rows = [jnp.sum(a, axis=0, keepdims=True) for a in arrays]
    rows.append(jnp.zeros((8 - len(rows), rows[0].shape[1]), jnp.float32))
    return jnp.concatenate(rows, axis=0)


KEY_SIZES = (256, 384, 512, 640, 768)
PAIR = 2 * HEAD_DIM


def key_size_cases(count, run):
    low = 0
    for size in KEY_SIZES:
        pl.when((count > low) & (count <= size))(partial(run, size))
        low = size


def split_heads(rows):
    first = lax.broadcasted_iota(jnp.int32, rows.shape, 1) < HEAD_DIM
    zero = jnp.zeros_like(rows)
    return jnp.concatenate([jnp.where(first, rows, zero), jnp.where(first, zero, rows)], axis=0)


def join_heads(both):
    kept = jnp.concatenate([both[:HEAD_DIM, :QUERY_BLOCK], both[HEAD_DIM:, QUERY_BLOCK:]], axis=0)
    return jnp.transpose(kept)


def mask_tail(values, count, other):
    size = values.shape[0]
    tail = values[size - 128 :]
    key_at = (size - 128) + lax.broadcasted_iota(jnp.int32, tail.shape, 0)
    return jnp.concatenate([values[: size - 128], jnp.where(key_at < count, tail, other)], axis=0)


def attend_kernel(unroll, info_ref, q_ref, k_ref, v_ref, mixture_ref, stats_ref, turned_ref):
    pairs = q_ref.shape[1] // PAIR
    mixture_ref[...] = jnp.zeros_like(mixture_ref)

    for seq in range(2):
        count = info_ref[seq]
        start = pl.multiple_of(info_ref[2 + seq], ROW_TILE)

        def run(size, seq=seq, count=count, start=start):
            keys = pl.ds(start, size)

            def some_pairs(step, carry):
                lanes = [pl.ds(pl.multiple_of((step * unroll + u) * PAIR, PAIR), PAIR) for u in range(unroll)]
                for u in range(unroll):
                    turned_ref[u, :, pl.ds(0, size)] = jnp.transpose(v_ref[keys, lanes[u]])

                def block(i, inner_carry):
                    row = pl.multiple_of(start + i * QUERY_BLOCK, ROW_TILE)
                    rows = pl.ds(row, QUERY_BLOCK)
                    for u in range(unroll):
                        q = split_heads(q_ref[rows, lanes[u]])
                        s = mask_tail(mm(k_ref[keys, lanes[u]], q, NT), count, -1e30)
                        top = jnp.max(s, axis=0, keepdims=True)
                        p = jnp.exp2((s - top) * (SCALE * LOG2E))
                        total = jnp.sum(p, axis=0, keepdims=True)
                        w = (p * (1.0 / total)).astype(jnp.bfloat16)
                        mixed = mm(turned_ref[u, :, pl.ds(0, size)], w)
                        mixture_ref[rows, lanes[u]] = join_heads(mixed).astype(jnp.bfloat16)
                        stats_ref[seq * 6 + i, pl.ds(step * unroll + u, 1), :] = top * (SCALE * LOG2E) + jnp.log2(total)
                    return inner_carry

                lax.fori_loop(0, pl.cdiv(count, QUERY_BLOCK), block, 0)
                return carry

            lax.fori_loop(0, pairs // unroll, some_pairs, 0)

        key_size_cases(count, run)


def attend(info, q, k, v, unroll=2):
    total, width = q.shape
    return pl.pallas_call(
        partial(attend_kernel, unroll),
        in_specs=[SMEM_WHOLE] + [VMEM_WHOLE] * 3,
        out_specs=[VMEM_WHOLE] * 2,
        out_shape=[
            sds((total, width), jnp.bfloat16),
            sds((12, 8, 2 * QUERY_BLOCK), jnp.float32),
        ],
        scratch_shapes=[pltpu.VMEM((unroll, PAIR, KEY_SIZES[-1]), jnp.bfloat16)],
        compiler_params=params(),
        cost_estimate=cost(15e9, 2e7, 8e6),
        name="attend",
    )(info, q, k, v)


def attend_back_kernel(unroll, first, info_ref, q_ref, k_ref, v_ref, stats_ref, g_ref, dq_ref, dk_ref, dv_ref, sums_ref, turned_ref, ak_ref, av_ref):
    pairs = dq_ref.shape[1] // PAIR
    sums_ref[...] = jnp.zeros_like(sums_ref)
    dq_ref[...] = jnp.zeros_like(dq_ref)
    dk_ref[...] = jnp.zeros_like(dk_ref)
    dv_ref[...] = jnp.zeros_like(dv_ref)

    for seq in range(2):
        count = info_ref[seq]
        start = pl.multiple_of(info_ref[2 + seq], ROW_TILE)

        def run(size, seq=seq, count=count, start=start):
            keys = pl.ds(start, size)
            here = pl.ds(0, size)

            def some_pairs(step, carry):
                lanes = [pl.ds(pl.multiple_of((first + step * unroll + u) * PAIR, PAIR), PAIR) for u in range(unroll)]
                to = [pl.ds(pl.multiple_of((step * unroll + u) * PAIR, PAIR), PAIR) for u in range(unroll)]
                for u in range(unroll):
                    turned_ref[u, :, here] = jnp.transpose(k_ref[keys, lanes[u]])
                    ak_ref[u, here, :] = jnp.zeros((size, PAIR), jnp.float32)
                    av_ref[u, here, :] = jnp.zeros((size, PAIR), jnp.float32)

                def block(i, inner_carry):
                    row = pl.multiple_of(start + i * QUERY_BLOCK, ROW_TILE)
                    rows = pl.ds(row, QUERY_BLOCK)
                    row_at = lax.broadcasted_iota(jnp.int32, (QUERY_BLOCK, PAIR), 0)
                    live = row_at < count - i * QUERY_BLOCK
                    for u in range(unroll):
                        q = split_heads(q_ref[rows, lanes[u]])
                        g = g_ref[rows, lanes[u]]
                        g = split_heads(jnp.where(live, g, jnp.zeros_like(g)))
                        stats = stats_ref[seq * 6 + i, pl.ds(first + step * unroll + u, 1), :]
                        s = mm(k_ref[keys, lanes[u]], q, NT) * (SCALE * LOG2E) - stats
                        w = jnp.exp2(mask_tail(s, count, -1e30))
                        dw = mm(v_ref[keys, lanes[u]], g, NT)
                        av_ref[u, here, :] += mm(w.astype(jnp.bfloat16), g)
                        inner = jnp.sum(w * dw, axis=0, keepdims=True)
                        ds = (w * (dw - inner)).astype(jnp.bfloat16)
                        ak_ref[u, here, :] += mm(ds, q)
                        dq = join_heads(mm(turned_ref[u, :, here], ds)) * SCALE
                        dq_ref[rows, to[u]] = dq.astype(jnp.bfloat16)
                        sums_ref[0:1, to[u]] += jnp.sum(dq, axis=0, keepdims=True)
                    return inner_carry

                lax.fori_loop(0, pl.cdiv(count, QUERY_BLOCK), block, 0)
                for u in range(unroll):
                    dk_ref[keys, to[u]] = (ak_ref[u, here, :] * SCALE).astype(jnp.bfloat16)
                    dv = av_ref[u, here, :]
                    dv_ref[keys, to[u]] = dv.astype(jnp.bfloat16)
                    sums_ref[1:2, to[u]] += jnp.sum(dv, axis=0, keepdims=True)
                return carry

            lax.fori_loop(0, pairs // unroll, some_pairs, 0)

        key_size_cases(count, run)


def attend_back(info, q, k, v, stats, g, first, pairs, unroll=2):
    total = q.shape[0]
    width = pairs * PAIR
    return pl.pallas_call(
        partial(attend_back_kernel, unroll, first),
        in_specs=[SMEM_WHOLE] + [VMEM_WHOLE] * 5,
        out_specs=[VMEM_WHOLE] * 4,
        out_shape=[sds((total, width), jnp.bfloat16)] * 3 + [sds((8, width), jnp.float32)],
        scratch_shapes=[
            pltpu.VMEM((unroll, PAIR, KEY_SIZES[-1]), jnp.bfloat16),
            pltpu.VMEM((unroll, KEY_SIZES[-1], PAIR), jnp.float32),
            pltpu.VMEM((unroll, KEY_SIZES[-1], PAIR), jnp.float32),
        ],
        compiler_params=params(),
        cost_estimate=cost(5e9 * pairs, 2e7, 1e6 * pairs),
        name="attend_back",
    )(info, q, k, v, stats, g)

BLOCK = 256
CHUNK = 128
MOST = 1536
TOTAL = MOST + SLACK


def pack_rows(info_ref, pair_ref, out_ref):
    slots = pair_ref.shape[1]
    out_ref[...] = jnp.zeros_like(out_ref)
    for seq in range(2):
        count = info_ref[seq]
        start = pl.multiple_of(info_ref[2 + seq], ROW_TILE)
        for at in range(0, slots, 128):
            size = min(128, slots - at)

            @pl.when(count > at)
            def _(seq=seq, at=at, size=size, count=count, start=start):
                rows = pair_ref[seq, pl.ds(at, size), :]
                row_at = at + lax.broadcasted_iota(jnp.int32, rows.shape, 0)
                rows = jnp.where(row_at < count, rows, jnp.bfloat16(0))
                out_ref[pl.ds(pl.multiple_of(start + at, ROW_TILE), size), :] = rows


def prepare_kernel(info_ref, pair_ref, gain_ref, shift_ref, x_ref, normed_ref):
    pack_rows(info_ref, pair_ref, x_ref)
    needed = info_ref[4]
    for at in range(0, TOTAL, 128):
        here = pl.ds(at, 128)

        @pl.when(at < needed)
        def _(here=here):
            unit, _ = norm_parts(x_ref[here, :].astype(jnp.float32))
            normed_ref[here, :] = (unit * gain_ref[...] + shift_ref[...]).astype(jnp.bfloat16)

        @pl.when(at >= needed)
        def _(here=here):
            normed_ref[here, :] = jnp.zeros((128, normed_ref.shape[1]), jnp.bfloat16)


def prepare(info, pair, gain, shift):
    width = pair.shape[2]
    return pl.pallas_call(
        prepare_kernel,
        in_specs=[SMEM_WHOLE] + [VMEM_WHOLE] * 3,
        out_specs=[VMEM_WHOLE] * 2,
        out_shape=[sds((TOTAL, width), jnp.bfloat16)] * 2,
        compiler_params=params(),
        cost_estimate=cost(0, 9e6),
        name="prepare",
    )(info, pair, gain, shift)


def pack(info, pair):
    return pl.pallas_call(
        pack_rows,
        in_specs=[SMEM_WHOLE, VMEM_WHOLE],
        out_specs=VMEM_WHOLE,
        out_shape=sds((MOST, pair.shape[2]), pair.dtype),
        compiler_params=params(),
        cost_estimate=cost(0, 5e6),
        name="pack",
    )(info, pair)


PIECES = 8


def exclusive(mask):
    return lambda value: lax.ppermute(
        value, "dp", [(i, i ^ mask) for i in range(lax.axis_size("dp"))]
    )


def across(mask):
    return lambda value: lax.ppermute(value, "tensor", [(i, i ^ mask) for i in range(4)])


def own_piece(rows, extra, place):
    count = rows.shape[0] // PIECES
    mine = lax.dynamic_slice_in_dim(rows, (place & (PIECES - 1)) * count, count).astype(jnp.float32)
    extra = jnp.pad(extra[None], ((0, 7), (0, rows.shape[1] - extra.shape[0])))
    return jnp.concatenate([mine, extra])


def spread_plane(own):
    return [own] + [exclusive(mask)(own) for mask in (2, 4, 6)]


def both_cores(four, *earlier):
    mine = jnp.concatenate([after(four[0], *earlier)] + four[1:] if earlier else four)
    return mine, exclusive(1)(mine)


def gather_out(w_out, place):
    half = w_out.shape[0] // 2
    mine = lax.dynamic_slice_in_dim(w_out, (place & 1) * half, half).astype(jnp.float32)
    mine = lax.all_gather(mine, "tensor")
    return mine, exclusive(1)(mine)


def place_pieces(place, mine_ref, other_ref, extra, to_ref, cast):
    rows = other_ref.shape[0] // 4 - extra
    for at in range(4):
        for core, ref in enumerate((mine_ref, other_ref)):
            to = pl.multiple_of((place ^ (2 * at + core)) * rows, 8)
            to_ref[pl.ds(to, rows), :] = cast(ref[at * (rows + extra) : at * (rows + extra) + rows, :])


def place_qkv_kernel(where_ref, own_ref, own_bias_ref, *rest):
    quarters, (w_ref, bias_ref, flat_ref) = rest[:6], rest[6:]
    width = w_ref.shape[1]
    local = own_ref.shape[0] // 3
    bias_ref[...] = jnp.zeros_like(bias_ref)
    for at in range(4):
        if at:
            mine, other = quarters[2 * at - 2 : 2 * at]
            place_pieces(where_ref[3], mine, other, 8, flat_ref, lambda piece: piece)
            rows = mine.shape[0] // 4 - 8
            biases = mine[rows : rows + 1, :]
        else:
            biases = own_bias_ref[...]
        for t in range(3):
            part = (flat_ref if at else own_ref)[t * local : (t + 1) * local, :]
            w_ref[t * width + at * local : t * width + (at + 1) * local, :] = part.astype(jnp.bfloat16)
        bias_ref[0:1, at * local : (at + 1) * local] = biases[:, 0:local]
        bias_ref[0:1, 2 * width + at * local : 2 * width + (at + 1) * local] = biases[:, local : 2 * local]


def place_qkv(where, own, own_bias, quarters):
    operands = [where, own, own_bias]
    for quarter in quarters:
        operands += quarter
    wide, width = own.shape
    return pl.pallas_call(
        place_qkv_kernel,
        in_specs=[SMEM_WHOLE] + [VMEM_WHOLE] * (len(operands) - 1),
        out_specs=[VMEM_WHOLE] * 2,
        out_shape=[sds((4 * wide, width), jnp.bfloat16), sds((8, 4 * wide), jnp.float32)],
        scratch_shapes=[pltpu.VMEM((wide, width), jnp.float32)],
        compiler_params=params(),
        cost_estimate=cost(0, 12e6),
        name="place_qkv",
    )(*operands)


def place_out_kernel(where_ref, mine_ref, theirs_ref, w_ref):
    half = mine_ref.shape[1]
    for at in range(4):
        for core in range(2):
            to = pl.multiple_of(at * 2 * half + (where_ref[1] ^ core) * half, ROW_TILE)
            from_ref = (mine_ref, theirs_ref)[core]
            w_ref[pl.ds(to, half), :] = from_ref[where_ref[0] ^ at].astype(jnp.bfloat16)


def place_out(where, mine, theirs):
    width = mine.shape[2]
    return pl.pallas_call(
        place_out_kernel,
        in_specs=[SMEM_WHOLE, VMEM_WHOLE, VMEM_WHOLE],
        out_specs=VMEM_WHOLE,
        out_shape=sds((8 * mine.shape[1], width), jnp.bfloat16),
        compiler_params=params(),
        cost_estimate=cost(0, 4e6),
        name="place_out",
    )(where, mine, theirs)


def live_block(width):
    return pl.BlockSpec((BLOCK, width), lambda i, where: (jnp.minimum(i, (where[2] - 1) // BLOCK), 0))


def every_block(width):
    return pl.BlockSpec((BLOCK, width), lambda i, where: (i, 0))


def fixed(shape):
    return pl.BlockSpec(shape, lambda i, where: (0,) * len(shape))


def project_kernel(where_ref, normed_ref, w_ref, bias_ref, *outs):
    width = normed_ref.shape[1]

    @pl.when(pl.program_id(0) * BLOCK < where_ref[2])
    def _():
        for t, out in enumerate(outs):
            here = slice(t * width, (t + 1) * width)
            out[...] = (mm(normed_ref[...], w_ref[here, :], NT) + bias_ref[0:1, here]).astype(jnp.bfloat16)

    @pl.when(pl.program_id(0) * BLOCK >= where_ref[2])
    def _():
        for out in outs:
            out[...] = jnp.zeros_like(out)


def project(where, normed, w, bias):
    width = normed.shape[1]
    return pl.pallas_call(
        project_kernel,
        grid_spec=pltpu.PrefetchScalarGridSpec(
            num_scalar_prefetch=1,
            grid=(TOTAL // BLOCK,),
            in_specs=[live_block(width), fixed(w.shape), fixed(bias.shape)],
            out_specs=[every_block(width)] * 3,
        ),
        out_shape=[sds((TOTAL, width), jnp.bfloat16)] * 3,
        compiler_params=params(),
        cost_estimate=cost(2 * 1024 * width * w.shape[0], 15e6),
        name="project",
    )(where, normed, w, bias)


def middle_kernel(where_ref, x_ref, mixture_ref, w_ref, vec_ref, hidden_ref, normed_ref):
    @pl.when(pl.program_id(0) * BLOCK < where_ref[2])
    def _():
        hidden = x_ref[...].astype(jnp.float32) + mm(mixture_ref[...], w_ref[...]) + vec_ref[0:1, :]
        row_at = pl.program_id(0) * BLOCK + lax.broadcasted_iota(jnp.int32, hidden.shape, 0)
        hidden = jnp.where(row_at < where_ref[2], hidden, 0.0)
        hidden_ref[...] = hidden
        unit, _ = norm_parts(hidden)
        normed_ref[...] = (unit * vec_ref[1:2, :] + vec_ref[2:3, :]).astype(jnp.bfloat16)


def middle(where, x, mixture, w, vec):
    width = x.shape[1]
    return pl.pallas_call(
        middle_kernel,
        grid_spec=pltpu.PrefetchScalarGridSpec(
            num_scalar_prefetch=1,
            grid=(MOST // BLOCK,),
            in_specs=[live_block(width), live_block(width), fixed(w.shape), fixed(vec.shape)],
            out_specs=[live_block(width)] * 2,
        ),
        out_shape=[sds((MOST, width), jnp.float32), sds((MOST, width), jnp.bfloat16)],
        compiler_params=params(),
        cost_estimate=cost(2 * 1024 * width * width, 1024 * width * 10),
        name="middle",
    )(where, x, mixture, w, vec)


def feed_forward(normed, g, w_up, b_up, w_down):
    up = mm(normed, w_up) + b_up
    cdf = 0.5 + 0.5 * lax.erf(up * (0.5**0.5))
    act = (up * cdf).astype(jnp.bfloat16)
    slope = cdf + up * (jnp.exp(-0.5 * up * up) * (1.0 / math.sqrt(2.0 * math.pi)))
    gup = mm(g, w_down, NT) * slope
    gul = gup.astype(jnp.bfloat16)
    return act, gup, gul, mm(act, w_down), mm(gul, w_up, NT)


def own_units_kernel(where_ref, normed_ref, g_ref, w_up_ref, b_up_ref, w_down_ref, *rest):
    down_ref, gmid_ref, grad_down_ref, grad_up_ref, sums_ref = rest

    @pl.when(pl.program_id(0) == 0)
    def _():
        grad_down_ref[...] = jnp.zeros_like(grad_down_ref)
        grad_up_ref[...] = jnp.zeros_like(grad_up_ref)
        sums_ref[...] = jnp.zeros_like(sums_ref)

    @pl.when(pl.program_id(0) * BLOCK < where_ref[2])
    def _():
        normed, g = normed_ref[...], g_ref[...]
        act, gup, gul, down, gmid = feed_forward(normed, g, w_up_ref[...], b_up_ref[...], w_down_ref[...])
        down_ref[...] = down
        gmid_ref[...] = gmid
        grad_down_ref[...] += mm(act, g, TN)
        grad_up_ref[...] += mm(normed, gul, TN)
        sums_ref[...] += column_sums(gup)


def own_units(where, normed, g, w_up, b_up, w_down):
    width, units = w_up.shape
    return pl.pallas_call(
        own_units_kernel,
        grid_spec=pltpu.PrefetchScalarGridSpec(
            num_scalar_prefetch=1,
            grid=(MOST // BLOCK,),
            in_specs=[
                live_block(width),
                live_block(width),
                fixed(w_up.shape),
                fixed(b_up.shape),
                fixed(w_down.shape),
            ],
            out_specs=[
                live_block(width),
                live_block(width),
                fixed((units, width)),
                fixed((width, units)),
                fixed((8, units)),
            ],
        ),
        out_shape=[
            sds((MOST, width), jnp.float32),
            sds((MOST, width), jnp.float32),
            sds((units, width), jnp.float32),
            sds((width, units), jnp.float32),
            sds((8, units), jnp.float32),
        ],
        compiler_params=params(),
        cost_estimate=cost(12 * 1024 * width * units, 25e6, 3e6),
        name="own_units",
    )(where, normed, g, w_up, b_up, w_down)


def place_weights(where_ref, mine_ref, other_ref, w_ref, b_ref):
    place_pieces(where_ref[3], mine_ref, other_ref, 8, w_ref, lambda piece: piece.astype(jnp.bfloat16))
    rows = mine_ref.shape[0] // 4 - 8
    b_ref[...] = mine_ref[rows : rows + 8, :]


def other_units_kernel(where_ref, mine_ref, other_ref, normed_ref, g_ref, *rest):
    down_in_ref, gmid_in_ref, down_ref, gmid_ref, w_ref, b_ref = rest
    width = normed_ref.shape[1]

    @pl.when(pl.program_id(0) == 0)
    def _():
        place_weights(where_ref, mine_ref, other_ref, w_ref, b_ref)

    @pl.when(pl.program_id(0) * BLOCK < where_ref[2])
    def _():
        _, _, _, down, gmid = feed_forward(
            normed_ref[...], g_ref[...], w_ref[0:width, :], b_ref[0:1, :], w_ref[width:, :]
        )
        down_ref[...] = down_in_ref[...] + down
        gmid_ref[...] = gmid_in_ref[...] + gmid


def other_units(where, quarter, normed, g, down, gmid):
    mine, other = quarter
    width = normed.shape[1]
    units = other.shape[1]
    return pl.pallas_call(
        other_units_kernel,
        grid_spec=pltpu.PrefetchScalarGridSpec(
            num_scalar_prefetch=1,
            grid=(MOST // BLOCK,),
            in_specs=[fixed(mine.shape), fixed(other.shape)] + [live_block(width)] * 4,
            out_specs=[live_block(width)] * 2,
            scratch_shapes=[pltpu.VMEM((2 * width, units), jnp.bfloat16), pltpu.VMEM((8, units), jnp.float32)],
        ),
        out_shape=[sds((MOST, width), jnp.float32)] * 2,
        input_output_aliases={5: 0, 6: 1},
        compiler_params=params(),
        cost_estimate=cost(8 * 1024 * width * units, 25e6, 3e6),
        name="other_units",
    )(where, mine, other, normed, g, down, gmid)


def last_units_kernel(where_ref, mine_ref, other_ref, normed_ref, g_ref, *rest):
    (down_in_ref, gmid_in_ref, hidden_ref, mixture_ref, vec_ref, w_out_ref) = rest[:6]
    (out_ref, gh_ref, gmix_ref, grad_w_out_ref, sums_ref, w_ref, b_ref) = rest[6:]
    width = normed_ref.shape[1]

    @pl.when(pl.program_id(0) == 0)
    def _():
        place_weights(where_ref, mine_ref, other_ref, w_ref, b_ref)
        grad_w_out_ref[...] = jnp.zeros_like(grad_w_out_ref)
        sums_ref[...] = jnp.zeros_like(sums_ref)

    @pl.when(pl.program_id(0) * BLOCK < where_ref[2])
    def _():
        g = g_ref[...]
        _, _, _, down, gmid = feed_forward(normed_ref[...], g, w_ref[0:width, :], b_ref[0:1, :], w_ref[width:, :])
        hidden = hidden_ref[...]
        out_ref[...] = (hidden + (down_in_ref[...] + down) + vec_ref[3:4, :]).astype(jnp.bfloat16)
        e = gmid_in_ref[...] + gmid
        unit, inverse = norm_parts(hidden)
        g = g.astype(jnp.float32)
        gh = g + norm_input_grad(e, unit, inverse, vec_ref[1:2, :])
        gh_ref[...] = gh
        ghl = gh.astype(jnp.bfloat16)
        gmix_ref[...] = mm(ghl, w_out_ref[...], NT).astype(jnp.bfloat16)
        grad_w_out_ref[...] += mm(mixture_ref[...], ghl, TN)[0 : grad_w_out_ref.shape[0], :]
        sums_ref[...] += column_sums(e * unit, e, gh, g)


def last_units(where, quarter, normed, g, down, gmid, hidden, mixture, vec, w_out, local):
    mine, other = quarter
    width = normed.shape[1]
    units = other.shape[1]
    return pl.pallas_call(
        last_units_kernel,
        grid_spec=pltpu.PrefetchScalarGridSpec(
            num_scalar_prefetch=1,
            grid=(MOST // BLOCK,),
            in_specs=[fixed(mine.shape), fixed(other.shape)]
            + [live_block(width)] * 5
            + [pl.BlockSpec((BLOCK, 2 * PAIR), lambda i, where: (jnp.minimum(i, (where[2] - 1) // BLOCK), 0))]
            + [fixed(vec.shape), fixed(w_out.shape)],
            out_specs=[
                live_block(width),
                live_block(width),
                live_block(width),
                fixed((local, width)),
                fixed((8, width)),
            ],
            scratch_shapes=[pltpu.VMEM((2 * width, units), jnp.bfloat16), pltpu.VMEM((8, units), jnp.float32)],
        ),
        out_shape=[
            sds((MOST, width), jnp.bfloat16),
            sds((MOST, width), jnp.float32),
            sds((TOTAL, width), jnp.bfloat16),
            sds((local, width), jnp.float32),
            sds((8, width), jnp.float32),
        ],
        compiler_params=params(),
        cost_estimate=cost(10 * 1024 * width * units, 35e6, 3e6),
        name="last_units",
    )(where, mine, other, normed, g, down, gmid, hidden, mixture, vec, w_out)


def own_grads_kernel(where_ref, dq_ref, dk_ref, dv_ref, normed_ref, *rest):
    grad_out_ref, up_ref, mid_ref, qv_ref, all_ref = rest
    local, width = grad_out_ref.shape

    @pl.when(pl.program_id(0) == 0)
    def _():
        all_ref[...] = jnp.zeros_like(all_ref)
        at = 3 * local
        for ref in (grad_out_ref, up_ref, mid_ref, qv_ref):
            all_ref[at : at + ref.shape[0], 0 : ref.shape[1]] = ref[...]
            at += ref.shape[0]

    @pl.when(pl.program_id(0) * BLOCK < where_ref[2])
    def _():
        for t, ref in enumerate((dq_ref, dk_ref, dv_ref)):
            here = slice(t * local, (t + 1) * local)
            all_ref[here, :] += mm(ref[...], normed_ref[...], TN)[0:local, :]


def own_grads(where, three, normed, *whole):
    local, width = whole[0].shape
    rows = 3 * local + sum(a.shape[0] for a in whole)
    rows = -(-rows // (8 * PIECES)) * 8 * PIECES
    return pl.pallas_call(
        own_grads_kernel,
        grid_spec=pltpu.PrefetchScalarGridSpec(
            num_scalar_prefetch=1,
            grid=(MOST // BLOCK,),
            in_specs=[live_block(a.shape[1]) for a in three]
            + [live_block(width)]
            + [fixed(a.shape) for a in whole],
            out_specs=fixed((rows, width)),
        ),
        out_shape=sds((rows, width), jnp.float32),
        compiler_params=params(),
        cost_estimate=cost(6 * 1024 * width * local, 12e6),
        name="own_grads",
    )(where, *three, normed, *whole)


def core_halves(rows, place):
    pieces = rows.reshape(4, 2, rows.shape[0] // PIECES, rows.shape[1])
    return [
        lax.dynamic_index_in_dim(pieces, core, 1, keepdims=False) for core in (place & 1, 1 - (place & 1))
    ]


def plane_sums(half, place):
    plane = (place >> 1) & 3
    pick = lambda at: lax.dynamic_index_in_dim(half, plane ^ at, 0, keepdims=False)
    return pick(0), [exclusive(2 * at)(pick(at)) for at in (1, 2, 3)]


def whole_sum(total):
    size = lax.axis_size("dp")
    if size > PIECES:
        groups = [list(range(i, size, PIECES)) for i in range(PIECES)]
        total = lax.psum(total, "dp", axis_index_groups=groups)
    return total


def place_sums_kernel(where_ref, mine_ref, other_ref, qkv_ref, out_ref, small_ref, all_ref):
    place_pieces(where_ref[3], mine_ref, other_ref, 0, all_ref, lambda piece: piece)
    at = 0
    for ref in (qkv_ref, out_ref, small_ref):
        ref[...] = all_ref[at : at + ref.shape[0], :]
        at += ref.shape[0]


def place_sums(where, mine, other, local):
    width = other.shape[1]
    return pl.pallas_call(
        place_sums_kernel,
        in_specs=[SMEM_WHOLE] + [VMEM_WHOLE] * 2,
        out_specs=[VMEM_WHOLE] * 3,
        out_shape=[sds((r, width), jnp.float32) for r in (3 * local, local, 24)],
        scratch_shapes=[pltpu.VMEM((2 * other.shape[0], width), jnp.float32)],
        compiler_params=params(),
        cost_estimate=cost(0, 6e6),
        name="place_sums",
    )(where, mine, other)


def in_back_kernel(where_ref, *refs):
    grads, (w_ref, x_ref, gh_ref, gain_ref, out_ref, sums_ref) = refs[:-6], refs[-6:]
    width = x_ref.shape[1]

    @pl.when(pl.program_id(0) == 0)
    def _():
        sums_ref[...] = jnp.zeros_like(sums_ref)

    @pl.when(pl.program_id(0) * BLOCK < where_ref[2])
    def _():
        e = 0.0
        for t in range(3):
            at = t * width
            for ref in grads[t::3]:
                e = e + mm(ref[...], w_ref[at : at + ref.shape[1], :])
                at += ref.shape[1]
        unit, inverse = norm_parts(x_ref[...].astype(jnp.float32))
        out_ref[...] = gh_ref[...] + norm_input_grad(e, unit, inverse, gain_ref[...])
        sums_ref[...] += column_sums(e * unit, e)


def in_back(where, shares, w, x, gh, gain):
    grads = [a for share in shares for a in share]
    width = x.shape[1]
    return pl.pallas_call(
        in_back_kernel,
        grid_spec=pltpu.PrefetchScalarGridSpec(
            num_scalar_prefetch=1,
            grid=(MOST // BLOCK,),
            in_specs=[live_block(a.shape[1]) for a in grads]
            + [fixed(w.shape), live_block(width), live_block(width), fixed(gain.shape)],
            out_specs=[live_block(width), fixed((8, width))],
        ),
        out_shape=[sds((TOTAL, width), jnp.float32), sds((8, width), jnp.float32)],
        compiler_params=params(),
        cost_estimate=cost(6 * 1024 * width * width, 20e6),
        name="in_back",
    )(where, *grads, w, x, gh, gain)


def unpack_kernel(info_ref, packed_ref, out_ref):
    slots = out_ref.shape[0]
    for seq in range(2):
        count = info_ref[seq]
        start = pl.multiple_of(info_ref[2 + seq], ROW_TILE)
        for at in range(0, slots, 128):
            size = min(128, slots - at)
            rows = packed_ref[pl.ds(pl.multiple_of(start + at, ROW_TILE), size), :]
            row_at = at + lax.broadcasted_iota(jnp.int32, rows.shape, 0)
            out_ref[pl.ds(at, size), seq, :] = jnp.where(row_at < count, rows, jnp.zeros_like(rows))


def unpack(info, packed, slots):
    width = packed.shape[1]
    out = pl.pallas_call(
        unpack_kernel,
        in_specs=[SMEM_WHOLE, VMEM_WHOLE],
        out_specs=VMEM_WHOLE,
        out_shape=sds((slots, 2, width), packed.dtype),
        compiler_params=params(),
        cost_estimate=cost(0, 10e6),
        name="unpack",
    )(info, packed)
    return out.transpose(1, 0, 2)


def shards(
    inputs,
    caption_lengths,
    g_attn,
    c_attn,
    w_qkv,
    b_qv,
    w_out,
    b_out,
    g_mlp,
    c_mlp,
    w_up,
    b_up,
    w_down,
    b_down,
    out_grad,
):
    seqs, slots, width = inputs.shape
    assert seqs == 2 and lax.axis_size("tensor") == 4 and lax.axis_size("dp") % PIECES == 0
    assert 2 * slots + ROW_TILE <= MOST
    local = w_qkv.shape[1]
    assert 4 * local == width and local <= 2 * PAIR
    place = lax.axis_index("dp")
    line_at = lax.axis_index("tensor")

    counts = jnp.minimum(caption_lengths + (IMAGE_ROWS + 1), slots)
    second_at = (counts[0] + (ROW_TILE - 1)) // ROW_TILE * ROW_TILE
    needed = second_at + counts[1]
    info = jnp.stack([counts[0], counts[1], jnp.int32(0), second_at, needed])
    where = jnp.stack([line_at, place & 1, needed, place & (PIECES - 1)])

    w_qkv_flat = w_qkv.reshape(3 * local, width)
    vec = jnp.concatenate([jnp.stack([b_out, g_mlp, c_mlp, b_down]), jnp.zeros((4, width), jnp.float32)])

    qkv_piece = own_piece(w_qkv_flat, b_qv.reshape(2 * local), place)
    units_piece = own_piece(jnp.concatenate([w_up, w_down]), b_up, place)
    x, normed_in = prepare(info, inputs, g_attn[None], c_attn[None])
    qkv_crossed = [across(d)(qkv_piece) for d in (1, 2, 3)]
    units_crossed = [across(d)(after(units_piece, normed_in)) for d in (1, 2, 3)]
    mine, theirs = gather_out(w_out, place)
    qkv_spread = [spread_plane(after(own, normed_in)) for own in qkv_crossed]
    g = pack(info, out_grad)
    qkv_quarters = [both_cores(four) for four in qkv_spread]
    own_bias = jnp.pad(b_qv.reshape(1, 2 * local), ((0, 0), (0, width - 2 * local)))
    w_qkv_all, bias = place_qkv(where, w_qkv_flat, own_bias, qkv_quarters)
    q, k, v = project(where, normed_in, w_qkv_all, bias)
    spread = [spread_plane(after(own, q)) for own in units_crossed[:2]]
    mixture, stats = attend(info, q, k, v, unroll=3)
    spread.append(spread_plane(after(units_crossed[2], mixture, g)))
    quarters = [both_cores(spread[0], mixture)]
    w_out_all = place_out(where, mine, theirs)
    hidden, normed_mid = middle(where, x, mixture, w_out_all, vec)
    quarters.append(both_cores(spread[1], hidden))
    down, gmid, grad_w_down, grad_w_up, up_sums = own_units(where, normed_mid, g, w_up, b_up[None], w_down)
    quarters.append(both_cores(spread[2], down))
    grad_w_down, grad_w_up = lax.psum((grad_w_down, grad_w_up), "dp")
    down, gmid = other_units(where, quarters[0], normed_mid, g, down, gmid)
    down, gmid = other_units(where, quarters[1], normed_mid, g, down, gmid)
    out, gh, gmix, grad_w_out, mid_sums = last_units(
        where, quarters[2], normed_mid, g, down, gmid, hidden, mixture, vec, w_out_all, local
    )
    *own, qv_sums = attend_back(info, q, k, v, stats, gmix, 0, 2)
    rest = own_grads(where, own, normed_in, grad_w_out, up_sums, mid_sums, qv_sums)
    kept, sent = core_halves(rest, place)
    got = exclusive(1)(sent)
    *some, _ = attend_back(info, q, k, v, stats, gmix, 2, 3, unroll=3)
    outputs = unpack(info, out, slots)
    kept, got = plane_sums(kept + after(got, some[0]), place)
    stats = after(stats, grad_w_down, grad_w_up, outputs)
    *others, _ = attend_back(info, q, k, v, stats, gmix, 5, 1, unroll=1)
    got = [after(a, others[0]) for a in got]
    got = spread_plane(whole_sum(kept + got[0] + got[1] + got[2]))
    back, in_sums = in_back(where, (own, some, others), w_qkv_all, x, gh, g_attn[None])
    rest = both_cores(got, in_sums)
    in_sums = whole_sum(in_sums + sum(exclusive(mask)(in_sums) for mask in (2, 4, 6)))
    in_sums = in_sums + exclusive(1)(in_sums)
    input_grad = unpack(info, back, slots)
    grad_w_qkv, grad_w_out, small = place_sums(where, *rest, local)
    up_sums, mid_sums, qv_sums = (small[8 * i : 8 * i + 8] for i in range(3))
    return (
        outputs,
        input_grad,
        in_sums[0],
        in_sums[1],
        grad_w_qkv.reshape(3, local, width),
        qv_sums[:2, :local],
        grad_w_out,
        mid_sums[2],
        mid_sums[0],
        mid_sums[1],
        grad_w_up,
        up_sums[0],
        grad_w_down,
        mid_sums[3],
    )


def solution(mesh):
    placed = (
        P("dp", None, None),
        P("dp"),
        P(),
        P(),
        P(None, "tensor", None),
        P(None, "tensor"),
        P("tensor", None),
        P(),
        P(),
        P(),
        P(None, "tensor"),
        P("tensor"),
        P("tensor", None),
        P(),
        P("dp", None, None),
    )
    return jax.shard_map(
        shards,
        mesh=mesh,
        in_specs=placed,
        out_specs=(
            P("dp", None, None),
            P("dp", None, None),
            P(),
            P(),
            P(None, "tensor", None),
            P(None, "tensor"),
            P("tensor", None),
            P(),
            P(),
            P(),
            P(None, "tensor"),
            P("tensor"),
            P("tensor", None),
            P(),
        ),
        check_vma=False,
    )
```

```python
import math
from functools import partial

import jax
import jax.numpy as jnp
from jax import lax
from jax.experimental import pallas as pl
from jax.experimental.pallas import tpu as pltpu
from jax.sharding import PartitionSpec as P

HEAD_DIM = 64
IMAGE_ROWS = 198
EPS = 1e-06
LOG2E = math.log2(math.e)
SCALE = HEAD_DIM ** (-0.5)
ROW_TILE = 16
QUERY_BLOCK = 256
BACK_BLOCK = 128
SLACK = 256
COST_SCALE = 0.02
VMEM_LIMIT = 48 * 1024 * 1024

NT = (((1,), (1,)), ((), ()))
TN = (((0,), (0,)), ((), ()))


def mm(a, b, dims=None):
    if dims is None:
        return jnp.dot(a, b, preferred_element_type=jnp.float32)
    return lax.dot_general(a, b, dims, preferred_element_type=jnp.float32)


def params():
    return pltpu.CompilerParams(vmem_limit_bytes=VMEM_LIMIT)


def cost(flops, moved, trans=0):
    scale = COST_SCALE
    return pl.CostEstimate(
        flops=int(flops * scale) + 1, bytes_accessed=int(moved * scale) + 1, transcendentals=int(trans * scale)
    )


def sds(shape, dtype):
    return jax.ShapeDtypeStruct(shape, dtype)


def after(value, *earlier):
    return lax.optimization_barrier((value,) + earlier)[0]


VMEM_WHOLE = pl.BlockSpec(memory_space=pltpu.VMEM)
SMEM_WHOLE = pl.BlockSpec(memory_space=pltpu.SMEM)


def norm_parts(values):
    average = jnp.mean(values, axis=-1, keepdims=True)
    centered = values - average
    squares = jnp.mean(centered * centered, axis=-1, keepdims=True)
    inverse = lax.rsqrt(squares + EPS)
    return centered * inverse, inverse


def norm_input_grad(grad_rows, unit_rows, inverse, gain):
    scaled = grad_rows * gain
    first = jnp.mean(scaled, axis=-1, keepdims=True)
    second = jnp.mean(scaled * unit_rows, axis=-1, keepdims=True)
    return inverse * (scaled - first - unit_rows * second)


def column_sums(*arrays):
    rows = [jnp.sum(a, axis=0, keepdims=True) for a in arrays]
    rows.append(jnp.zeros((8 - len(rows), rows[0].shape[1]), jnp.float32))
    return jnp.concatenate(rows, axis=0)


KEY_SIZES = (256, 384, 512, 640, 768)
PAIR = 2 * HEAD_DIM
STAT_BLOCKS = KEY_SIZES[-1] // QUERY_BLOCK


def key_size_cases(count, run):
    low = 0
    for size in KEY_SIZES:
        pl.when((count > low) & (count <= size))(partial(run, size))
        low = size


def split_heads(rows):
    first = lax.broadcasted_iota(jnp.int32, rows.shape, 1) < HEAD_DIM
    zero = jnp.zeros_like(rows)
    return jnp.concatenate([jnp.where(first, rows, zero), jnp.where(first, zero, rows)], axis=0)


def join_heads(both):
    kept = jnp.concatenate([both[:HEAD_DIM, :BACK_BLOCK], both[HEAD_DIM:, BACK_BLOCK:]], axis=0)
    return jnp.transpose(kept)


def pick_heads(both):
    first = lax.broadcasted_iota(jnp.int32, (QUERY_BLOCK, PAIR), 1) < HEAD_DIM
    return jnp.where(first, both[:QUERY_BLOCK], both[QUERY_BLOCK:])


def mask_tail(values, count, other):
    size = values.shape[0]
    tail = values[size - 128 :]
    key_at = (size - 128) + lax.broadcasted_iota(jnp.int32, tail.shape, 0)
    return jnp.concatenate([values[: size - 128], jnp.where(key_at < count, tail, other)], axis=0)


def attend_kernel(unroll, info_ref, q_ref, k_ref, v_ref, mixture_ref, stats_ref):
    pairs = q_ref.shape[1] // PAIR
    mixture_ref[...] = jnp.zeros_like(mixture_ref)

    for seq in range(2):
        count = info_ref[seq]
        start = pl.multiple_of(info_ref[2 + seq], ROW_TILE)

        def run(size, seq=seq, count=count, start=start):
            keys = pl.ds(start, size)

            def some_pairs(step, carry):
                lanes = [pl.ds(pl.multiple_of((step * unroll + u) * PAIR, PAIR), PAIR) for u in range(unroll)]

                def block(i, inner_carry):
                    rows = pl.ds(pl.multiple_of(start + i * QUERY_BLOCK, ROW_TILE), QUERY_BLOCK)
                    at = lax.broadcasted_iota(jnp.int32, (2 * QUERY_BLOCK, PAIR), 1)
                    stats = jnp.zeros((2 * QUERY_BLOCK, PAIR), jnp.float32)
                    for u in range(unroll):
                        q = split_heads(q_ref[rows, lanes[u]])
                        s = mm(q, k_ref[keys, lanes[u]], NT)
                        tail = s[:, size - 128 :]
                        key_at = (size - 128) + lax.broadcasted_iota(jnp.int32, tail.shape, 1)
                        tail = jnp.where(key_at < count, tail, -1e30)
                        s = jnp.concatenate([s[:, : size - 128], tail], axis=1)
                        top = jnp.max(s, axis=1, keepdims=True)
                        p = jnp.exp2((s - top) * (SCALE * LOG2E))
                        total = jnp.sum(p, axis=1, keepdims=True)
                        mixed = mm(p.astype(jnp.bfloat16), v_ref[keys, lanes[u]]) * (1.0 / total)
                        mixture_ref[rows, lanes[u]] = pick_heads(mixed).astype(jnp.bfloat16)
                        stats = jnp.where(at == u, top * (SCALE * LOG2E) + jnp.log2(total), stats)
                    stats = jnp.transpose(stats)
                    for u in range(unroll):
                        stats_ref[seq * STAT_BLOCKS + i, pl.ds(step * unroll + u, 1), :] = stats[u : u + 1, :]
                    return inner_carry

                lax.fori_loop(0, pl.cdiv(count, QUERY_BLOCK), block, 0)
                return carry

            lax.fori_loop(0, pairs // unroll, some_pairs, 0)

        key_size_cases(count, run)


def attend(info, q, k, v, unroll=2):
    total, width = q.shape
    return pl.pallas_call(
        partial(attend_kernel, unroll),
        in_specs=[SMEM_WHOLE] + [VMEM_WHOLE] * 3,
        out_specs=[VMEM_WHOLE] * 2,
        out_shape=[
            sds((total, width), jnp.bfloat16),
            sds((2 * STAT_BLOCKS, 8, 2 * QUERY_BLOCK), jnp.float32),
        ],
        compiler_params=params(),
        cost_estimate=cost(15e9, 2e7, 8e6),
        name="attend",
    )(info, q, k, v)


def attend_back_kernel(unroll, first, first_stat, info_ref, q_ref, k_ref, v_ref, stats_ref, g_ref, dq_ref, dk_ref, dv_ref, sums_ref, turned_ref, ak_ref, av_ref):
    pairs = dq_ref.shape[1] // PAIR
    sums_ref[...] = jnp.zeros_like(sums_ref)
    dq_ref[...] = jnp.zeros_like(dq_ref)
    dk_ref[...] = jnp.zeros_like(dk_ref)
    dv_ref[...] = jnp.zeros_like(dv_ref)

    for seq in range(2):
        count = info_ref[seq]
        start = pl.multiple_of(info_ref[2 + seq], ROW_TILE)

        def run(size, seq=seq, count=count, start=start):
            keys = pl.ds(start, size)
            here = pl.ds(0, size)

            def some_pairs(step, carry):
                lanes = [pl.ds(pl.multiple_of((first + step * unroll + u) * PAIR, PAIR), PAIR) for u in range(unroll)]
                to = [pl.ds(pl.multiple_of((step * unroll + u) * PAIR, PAIR), PAIR) for u in range(unroll)]
                for u in range(unroll):
                    turned_ref[u, :, here] = jnp.transpose(k_ref[keys, lanes[u]])
                    ak_ref[u, here, :] = jnp.zeros((size, PAIR), jnp.float32)
                    av_ref[u, here, :] = jnp.zeros((size, PAIR), jnp.float32)

                def block(i, inner_carry):
                    row = pl.multiple_of(start + i * BACK_BLOCK, ROW_TILE)
                    rows = pl.ds(row, BACK_BLOCK)
                    row_at = lax.broadcasted_iota(jnp.int32, (BACK_BLOCK, PAIR), 0)
                    live = row_at < count - i * BACK_BLOCK
                    for u in range(unroll):
                        q = split_heads(q_ref[rows, lanes[u]])
                        g = g_ref[rows, lanes[u]]
                        g = split_heads(jnp.where(live, g, jnp.zeros_like(g)))
                        half = pl.multiple_of((i & 1) * BACK_BLOCK, BACK_BLOCK)
                        at = (seq * STAT_BLOCKS + (i >> 1), pl.ds(first_stat + step * unroll + u, 1))
                        stats = [stats_ref[(*at, pl.ds(h + half, BACK_BLOCK))] for h in (0, QUERY_BLOCK)]
                        stats = jnp.concatenate(stats, axis=1)
                        s = mm(k_ref[keys, lanes[u]], q, NT) * (SCALE * LOG2E) - stats
                        w = jnp.exp2(mask_tail(s, count, -1e30))
                        dw = mm(v_ref[keys, lanes[u]], g, NT)
                        av_ref[u, here, :] += mm(w.astype(jnp.bfloat16), g)
                        inner = jnp.sum(w * dw, axis=0, keepdims=True)
                        ds = (w * (dw - inner)).astype(jnp.bfloat16)
                        ak_ref[u, here, :] += mm(ds, q)
                        dq = join_heads(mm(turned_ref[u, :, here], ds)) * SCALE
                        dq_ref[rows, to[u]] = dq.astype(jnp.bfloat16)
                        sums_ref[0:1, to[u]] += jnp.sum(dq, axis=0, keepdims=True)
                    return inner_carry

                lax.fori_loop(0, pl.cdiv(count, BACK_BLOCK), block, 0)
                for u in range(unroll):
                    dk_ref[keys, to[u]] = (ak_ref[u, here, :] * SCALE).astype(jnp.bfloat16)
                    dv = av_ref[u, here, :]
                    dv_ref[keys, to[u]] = dv.astype(jnp.bfloat16)
                    sums_ref[1:2, to[u]] += jnp.sum(dv, axis=0, keepdims=True)
                return carry

            lax.fori_loop(0, pairs // unroll, some_pairs, 0)

        key_size_cases(count, run)


def attend_back(info, q, k, v, stats, g, first, pairs, first_stat, unroll=2):
    total = q.shape[0]
    width = pairs * PAIR
    return pl.pallas_call(
        partial(attend_back_kernel, unroll, first, first_stat),
        in_specs=[SMEM_WHOLE] + [VMEM_WHOLE] * 5,
        out_specs=[VMEM_WHOLE] * 4,
        out_shape=[sds((total, width), jnp.bfloat16)] * 3 + [sds((8, width), jnp.float32)],
        scratch_shapes=[
            pltpu.VMEM((unroll, PAIR, KEY_SIZES[-1]), jnp.bfloat16),
            pltpu.VMEM((unroll, KEY_SIZES[-1], PAIR), jnp.float32),
            pltpu.VMEM((unroll, KEY_SIZES[-1], PAIR), jnp.float32),
        ],
        compiler_params=params(),
        cost_estimate=cost(5e9 * pairs, 2e7, 1e6 * pairs),
        name="attend_back",
    )(info, q, k, v, stats, g)

BLOCK = 256
CHUNK = 128
MOST = 1536
TOTAL = MOST + SLACK


def pack_rows(info_ref, pair_ref, out_ref):
    slots = pair_ref.shape[1]
    out_ref[...] = jnp.zeros_like(out_ref)
    for seq in range(2):
        count = info_ref[seq]
        start = pl.multiple_of(info_ref[2 + seq], ROW_TILE)
        for at in range(0, slots, 128):
            size = min(128, slots - at)

            @pl.when(count > at)
            def _(seq=seq, at=at, size=size, count=count, start=start):
                rows = pair_ref[seq, pl.ds(at, size), :]
                row_at = at + lax.broadcasted_iota(jnp.int32, rows.shape, 0)
                rows = jnp.where(row_at < count, rows, jnp.bfloat16(0))
                out_ref[pl.ds(pl.multiple_of(start + at, ROW_TILE), size), :] = rows


def prepare_kernel(info_ref, pair_ref, gain_ref, shift_ref, x_ref, normed_ref):
    pack_rows(info_ref, pair_ref, x_ref)
    needed = info_ref[4]
    for at in range(0, TOTAL, 128):
        here = pl.ds(at, 128)

        @pl.when(at < needed)
        def _(here=here):
            unit, _ = norm_parts(x_ref[here, :].astype(jnp.float32))
            normed_ref[here, :] = (unit * gain_ref[...] + shift_ref[...]).astype(jnp.bfloat16)

        @pl.when(at >= needed)
        def _(here=here):
            normed_ref[here, :] = jnp.zeros((128, normed_ref.shape[1]), jnp.bfloat16)


def prepare(info, pair, gain, shift):
    width = pair.shape[2]
    return pl.pallas_call(
        prepare_kernel,
        in_specs=[SMEM_WHOLE] + [VMEM_WHOLE] * 3,
        out_specs=[VMEM_WHOLE] * 2,
        out_shape=[sds((TOTAL, width), jnp.bfloat16)] * 2,
        compiler_params=params(),
        cost_estimate=cost(0, 9e6),
        name="prepare",
    )(info, pair, gain, shift)


def pack(info, pair):
    return pl.pallas_call(
        pack_rows,
        in_specs=[SMEM_WHOLE, VMEM_WHOLE],
        out_specs=VMEM_WHOLE,
        out_shape=sds((MOST, pair.shape[2]), pair.dtype),
        compiler_params=params(),
        cost_estimate=cost(0, 5e6),
        name="pack",
    )(info, pair)


PIECES = 8


def exclusive(mask):
    return lambda value: lax.ppermute(
        value, "dp", [(i, i ^ mask) for i in range(lax.axis_size("dp"))]
    )


def across(mask):
    return lambda value: lax.ppermute(value, "tensor", [(i, i ^ mask) for i in range(4)])


def own_piece(rows, extra, place):
    count = rows.shape[0] // PIECES
    mine = lax.dynamic_slice_in_dim(rows, (place & (PIECES - 1)) * count, count).astype(jnp.float32)
    extra = jnp.pad(extra[None], ((0, 7), (0, rows.shape[1] - extra.shape[0])))
    return jnp.concatenate([mine, extra])


def spread_plane(own):
    return [own] + [exclusive(mask)(own) for mask in (2, 4, 6)]


def both_cores(four, *earlier):
    mine = jnp.concatenate([after(four[0], *earlier)] + four[1:] if earlier else four)
    return mine, exclusive(1)(mine)


def gather_out(w_out, place):
    half = w_out.shape[0] // 2
    mine = lax.dynamic_slice_in_dim(w_out, (place & 1) * half, half).astype(jnp.float32)
    mine = lax.all_gather(mine, "tensor")
    return mine, exclusive(1)(mine)


def place_pieces(place, mine_ref, other_ref, extra, to_ref, cast):
    rows = other_ref.shape[0] // 4 - extra
    for at in range(4):
        for core, ref in enumerate((mine_ref, other_ref)):
            to = pl.multiple_of((place ^ (2 * at + core)) * rows, 8)
            to_ref[pl.ds(to, rows), :] = cast(ref[at * (rows + extra) : at * (rows + extra) + rows, :])


def place_qkv_kernel(where_ref, own_ref, own_bias_ref, *rest):
    quarters, (w_ref, bias_ref, flat_ref) = rest[:6], rest[6:]
    width = w_ref.shape[1]
    local = own_ref.shape[0] // 3
    bias_ref[...] = jnp.zeros_like(bias_ref)
    for at in range(4):
        if at:
            mine, other = quarters[2 * at - 2 : 2 * at]
            place_pieces(where_ref[3], mine, other, 8, flat_ref, lambda piece: piece)
            rows = mine.shape[0] // 4 - 8
            biases = mine[rows : rows + 1, :]
        else:
            biases = own_bias_ref[...]
        for t in range(3):
            part = (flat_ref if at else own_ref)[t * local : (t + 1) * local, :]
            w_ref[t * width + at * local : t * width + (at + 1) * local, :] = part.astype(jnp.bfloat16)
        bias_ref[0:1, at * local : (at + 1) * local] = biases[:, 0:local]
        bias_ref[0:1, 2 * width + at * local : 2 * width + (at + 1) * local] = biases[:, local : 2 * local]


def place_qkv(where, own, own_bias, quarters):
    operands = [where, own, own_bias]
    for quarter in quarters:
        operands += quarter
    wide, width = own.shape
    return pl.pallas_call(
        place_qkv_kernel,
        in_specs=[SMEM_WHOLE] + [VMEM_WHOLE] * (len(operands) - 1),
        out_specs=[VMEM_WHOLE] * 2,
        out_shape=[sds((4 * wide, width), jnp.bfloat16), sds((8, 4 * wide), jnp.float32)],
        scratch_shapes=[pltpu.VMEM((wide, width), jnp.float32)],
        compiler_params=params(),
        cost_estimate=cost(0, 12e6),
        name="place_qkv",
    )(*operands)


def place_out_kernel(where_ref, mine_ref, theirs_ref, w_ref):
    half = mine_ref.shape[1]
    for at in range(4):
        for core in range(2):
            to = pl.multiple_of(at * 2 * half + (where_ref[1] ^ core) * half, ROW_TILE)
            from_ref = (mine_ref, theirs_ref)[core]
            w_ref[pl.ds(to, half), :] = from_ref[where_ref[0] ^ at].astype(jnp.bfloat16)


def place_out(where, mine, theirs):
    width = mine.shape[2]
    return pl.pallas_call(
        place_out_kernel,
        in_specs=[SMEM_WHOLE, VMEM_WHOLE, VMEM_WHOLE],
        out_specs=VMEM_WHOLE,
        out_shape=sds((8 * mine.shape[1], width), jnp.bfloat16),
        compiler_params=params(),
        cost_estimate=cost(0, 4e6),
        name="place_out",
    )(where, mine, theirs)


def live_block(width):
    return pl.BlockSpec((BLOCK, width), lambda i, where: (jnp.minimum(i, (where[2] - 1) // BLOCK), 0))


def every_block(width):
    return pl.BlockSpec((BLOCK, width), lambda i, where: (i, 0))


def fixed(shape):
    return pl.BlockSpec(shape, lambda i, where: (0,) * len(shape))


def project_kernel(where_ref, normed_ref, w_ref, bias_ref, *outs):
    width = normed_ref.shape[1]

    @pl.when(pl.program_id(0) * BLOCK < where_ref[2])
    def _():
        for t, out in enumerate(outs):
            here = slice(t * width, (t + 1) * width)
            out[...] = (mm(normed_ref[...], w_ref[here, :], NT) + bias_ref[0:1, here]).astype(jnp.bfloat16)

    @pl.when(pl.program_id(0) * BLOCK >= where_ref[2])
    def _():
        for out in outs:
            out[...] = jnp.zeros_like(out)


def project(where, normed, w, bias):
    width = normed.shape[1]
    return pl.pallas_call(
        project_kernel,
        grid_spec=pltpu.PrefetchScalarGridSpec(
            num_scalar_prefetch=1,
            grid=(TOTAL // BLOCK,),
            in_specs=[live_block(width), fixed(w.shape), fixed(bias.shape)],
            out_specs=[every_block(width)] * 3,
        ),
        out_shape=[sds((TOTAL, width), jnp.bfloat16)] * 3,
        compiler_params=params(),
        cost_estimate=cost(2 * 1024 * width * w.shape[0], 15e6),
        name="project",
    )(where, normed, w, bias)


def middle_kernel(where_ref, x_ref, mixture_ref, w_ref, vec_ref, hidden_ref, normed_ref):
    @pl.when(pl.program_id(0) * BLOCK < where_ref[2])
    def _():
        hidden = x_ref[...].astype(jnp.float32) + mm(mixture_ref[...], w_ref[...]) + vec_ref[0:1, :]
        row_at = pl.program_id(0) * BLOCK + lax.broadcasted_iota(jnp.int32, hidden.shape, 0)
        hidden = jnp.where(row_at < where_ref[2], hidden, 0.0)
        hidden_ref[...] = hidden
        unit, _ = norm_parts(hidden)
        normed_ref[...] = (unit * vec_ref[1:2, :] + vec_ref[2:3, :]).astype(jnp.bfloat16)


def middle(where, x, mixture, w, vec):
    width = x.shape[1]
    return pl.pallas_call(
        middle_kernel,
        grid_spec=pltpu.PrefetchScalarGridSpec(
            num_scalar_prefetch=1,
            grid=(MOST // BLOCK,),
            in_specs=[live_block(width), live_block(width), fixed(w.shape), fixed(vec.shape)],
            out_specs=[live_block(width)] * 2,
        ),
        out_shape=[sds((MOST, width), jnp.float32), sds((MOST, width), jnp.bfloat16)],
        compiler_params=params(),
        cost_estimate=cost(2 * 1024 * width * width, 1024 * width * 10),
        name="middle",
    )(where, x, mixture, w, vec)


def feed_forward(normed, g, w_up, b_up, w_down):
    up = mm(normed, w_up) + b_up
    cdf = 0.5 + 0.5 * lax.erf(up * (0.5**0.5))
    act = (up * cdf).astype(jnp.bfloat16)
    slope = cdf + up * (jnp.exp(-0.5 * up * up) * (1.0 / math.sqrt(2.0 * math.pi)))
    gup = mm(g, w_down, NT) * slope
    gul = gup.astype(jnp.bfloat16)
    return act, gup, gul, mm(act, w_down), mm(gul, w_up, NT)


def own_units_kernel(where_ref, normed_ref, g_ref, w_up_ref, b_up_ref, w_down_ref, *rest):
    down_ref, gmid_ref, grad_down_ref, grad_up_ref, sums_ref = rest

    @pl.when(pl.program_id(0) == 0)
    def _():
        grad_down_ref[...] = jnp.zeros_like(grad_down_ref)
        grad_up_ref[...] = jnp.zeros_like(grad_up_ref)
        sums_ref[...] = jnp.zeros_like(sums_ref)

    @pl.when(pl.program_id(0) * BLOCK < where_ref[2])
    def _():
        normed, g = normed_ref[...], g_ref[...]
        act, gup, gul, down, gmid = feed_forward(normed, g, w_up_ref[...], b_up_ref[...], w_down_ref[...])
        down_ref[...] = down
        gmid_ref[...] = gmid
        grad_down_ref[...] += mm(act, g, TN)
        grad_up_ref[...] += mm(normed, gul, TN)
        sums_ref[...] += column_sums(gup)


def own_units(where, normed, g, w_up, b_up, w_down):
    width, units = w_up.shape
    return pl.pallas_call(
        own_units_kernel,
        grid_spec=pltpu.PrefetchScalarGridSpec(
            num_scalar_prefetch=1,
            grid=(MOST // BLOCK,),
            in_specs=[
                live_block(width),
                live_block(width),
                fixed(w_up.shape),
                fixed(b_up.shape),
                fixed(w_down.shape),
            ],
            out_specs=[
                live_block(width),
                live_block(width),
                fixed((units, width)),
                fixed((width, units)),
                fixed((8, units)),
            ],
        ),
        out_shape=[
            sds((MOST, width), jnp.float32),
            sds((MOST, width), jnp.float32),
            sds((units, width), jnp.float32),
            sds((width, units), jnp.float32),
            sds((8, units), jnp.float32),
        ],
        compiler_params=params(),
        cost_estimate=cost(12 * 1024 * width * units, 25e6, 3e6),
        name="own_units",
    )(where, normed, g, w_up, b_up, w_down)


def place_weights(where_ref, mine_ref, other_ref, w_ref, b_ref):
    place_pieces(where_ref[3], mine_ref, other_ref, 8, w_ref, lambda piece: piece.astype(jnp.bfloat16))
    rows = mine_ref.shape[0] // 4 - 8
    b_ref[...] = mine_ref[rows : rows + 8, :]


def other_units_kernel(where_ref, mine_ref, other_ref, normed_ref, g_ref, *rest):
    down_in_ref, gmid_in_ref, down_ref, gmid_ref, w_ref, b_ref = rest
    width = normed_ref.shape[1]

    @pl.when(pl.program_id(0) == 0)
    def _():
        place_weights(where_ref, mine_ref, other_ref, w_ref, b_ref)

    @pl.when(pl.program_id(0) * BLOCK < where_ref[2])
    def _():
        _, _, _, down, gmid = feed_forward(
            normed_ref[...], g_ref[...], w_ref[0:width, :], b_ref[0:1, :], w_ref[width:, :]
        )
        down_ref[...] = down_in_ref[...] + down
        gmid_ref[...] = gmid_in_ref[...] + gmid


def other_units(where, quarter, normed, g, down, gmid):
    mine, other = quarter
    width = normed.shape[1]
    units = other.shape[1]
    return pl.pallas_call(
        other_units_kernel,
        grid_spec=pltpu.PrefetchScalarGridSpec(
            num_scalar_prefetch=1,
            grid=(MOST // BLOCK,),
            in_specs=[fixed(mine.shape), fixed(other.shape)] + [live_block(width)] * 4,
            out_specs=[live_block(width)] * 2,
            scratch_shapes=[pltpu.VMEM((2 * width, units), jnp.bfloat16), pltpu.VMEM((8, units), jnp.float32)],
        ),
        out_shape=[sds((MOST, width), jnp.float32)] * 2,
        input_output_aliases={5: 0, 6: 1},
        compiler_params=params(),
        cost_estimate=cost(8 * 1024 * width * units, 25e6, 3e6),
        name="other_units",
    )(where, mine, other, normed, g, down, gmid)


def last_units_kernel(where_ref, mine_ref, other_ref, normed_ref, g_ref, *rest):
    (down_in_ref, gmid_in_ref, hidden_ref, mixture_ref, vec_ref, w_out_ref) = rest[:6]
    (out_ref, gh_ref, gmix_ref, grad_w_out_ref, sums_ref, w_ref, b_ref) = rest[6:]
    width = normed_ref.shape[1]

    @pl.when(pl.program_id(0) == 0)
    def _():
        place_weights(where_ref, mine_ref, other_ref, w_ref, b_ref)
        grad_w_out_ref[...] = jnp.zeros_like(grad_w_out_ref)
        sums_ref[...] = jnp.zeros_like(sums_ref)

    @pl.when(pl.program_id(0) * BLOCK < where_ref[2])
    def _():
        g = g_ref[...]
        _, _, _, down, gmid = feed_forward(normed_ref[...], g, w_ref[0:width, :], b_ref[0:1, :], w_ref[width:, :])
        hidden = hidden_ref[...]
        out_ref[...] = (hidden + (down_in_ref[...] + down) + vec_ref[3:4, :]).astype(jnp.bfloat16)
        e = gmid_in_ref[...] + gmid
        unit, inverse = norm_parts(hidden)
        g = g.astype(jnp.float32)
        gh = g + norm_input_grad(e, unit, inverse, vec_ref[1:2, :])
        gh_ref[...] = gh
        ghl = gh.astype(jnp.bfloat16)
        gmix_ref[...] = mm(ghl, w_out_ref[...], NT).astype(jnp.bfloat16)
        grad_w_out_ref[...] += mm(mixture_ref[...], ghl, TN)[0 : grad_w_out_ref.shape[0], :]
        sums_ref[...] += column_sums(e * unit, e, gh, g)


def last_units(where, quarter, normed, g, down, gmid, hidden, mixture, vec, w_out, local):
    mine, other = quarter
    width = normed.shape[1]
    units = other.shape[1]
    return pl.pallas_call(
        last_units_kernel,
        grid_spec=pltpu.PrefetchScalarGridSpec(
            num_scalar_prefetch=1,
            grid=(MOST // BLOCK,),
            in_specs=[fixed(mine.shape), fixed(other.shape)]
            + [live_block(width)] * 5
            + [pl.BlockSpec((BLOCK, 2 * PAIR), lambda i, where: (jnp.minimum(i, (where[2] - 1) // BLOCK), 0))]
            + [fixed(vec.shape), fixed(w_out.shape)],
            out_specs=[
                live_block(width),
                live_block(width),
                live_block(width),
                fixed((local, width)),
                fixed((8, width)),
            ],
            scratch_shapes=[pltpu.VMEM((2 * width, units), jnp.bfloat16), pltpu.VMEM((8, units), jnp.float32)],
        ),
        out_shape=[
            sds((MOST, width), jnp.bfloat16),
            sds((MOST, width), jnp.float32),
            sds((TOTAL, width), jnp.bfloat16),
            sds((local, width), jnp.float32),
            sds((8, width), jnp.float32),
        ],
        compiler_params=params(),
        cost_estimate=cost(10 * 1024 * width * units, 35e6, 3e6),
        name="last_units",
    )(where, mine, other, normed, g, down, gmid, hidden, mixture, vec, w_out)


def own_grads_kernel(where_ref, dq_ref, dk_ref, dv_ref, normed_ref, *rest):
    grad_out_ref, up_ref, mid_ref, qv_ref, all_ref = rest
    local, width = grad_out_ref.shape

    @pl.when(pl.program_id(0) == 0)
    def _():
        all_ref[...] = jnp.zeros_like(all_ref)
        at = 3 * local
        for ref in (grad_out_ref, up_ref, mid_ref, qv_ref):
            all_ref[at : at + ref.shape[0], 0 : ref.shape[1]] = ref[...]
            at += ref.shape[0]

    @pl.when(pl.program_id(0) * BLOCK < where_ref[2])
    def _():
        for t, ref in enumerate((dq_ref, dk_ref, dv_ref)):
            here = slice(t * local, (t + 1) * local)
            all_ref[here, :] += mm(ref[...], normed_ref[...], TN)[0:local, :]


def own_grads(where, three, normed, *whole):
    local, width = whole[0].shape
    rows = 3 * local + sum(a.shape[0] for a in whole)
    rows = -(-rows // (8 * PIECES)) * 8 * PIECES
    return pl.pallas_call(
        own_grads_kernel,
        grid_spec=pltpu.PrefetchScalarGridSpec(
            num_scalar_prefetch=1,
            grid=(MOST // BLOCK,),
            in_specs=[live_block(a.shape[1]) for a in three]
            + [live_block(width)]
            + [fixed(a.shape) for a in whole],
            out_specs=fixed((rows, width)),
        ),
        out_shape=sds((rows, width), jnp.float32),
        compiler_params=params(),
        cost_estimate=cost(6 * 1024 * width * local, 12e6),
        name="own_grads",
    )(where, *three, normed, *whole)


def core_halves(rows, place):
    pieces = rows.reshape(4, 2, rows.shape[0] // PIECES, rows.shape[1])
    return [
        lax.dynamic_index_in_dim(pieces, core, 1, keepdims=False) for core in (place & 1, 1 - (place & 1))
    ]


def plane_sums(half, place):
    plane = (place >> 1) & 3
    pick = lambda at: lax.dynamic_index_in_dim(half, plane ^ at, 0, keepdims=False)
    return pick(0), [exclusive(2 * at)(pick(at)) for at in (1, 2, 3)]


def whole_sum(total):
    size = lax.axis_size("dp")
    if size > PIECES:
        groups = [list(range(i, size, PIECES)) for i in range(PIECES)]
        total = lax.psum(total, "dp", axis_index_groups=groups)
    return total


def place_sums_kernel(where_ref, mine_ref, other_ref, qkv_ref, out_ref, small_ref, all_ref):
    place_pieces(where_ref[3], mine_ref, other_ref, 0, all_ref, lambda piece: piece)
    at = 0
    for ref in (qkv_ref, out_ref, small_ref):
        ref[...] = all_ref[at : at + ref.shape[0], :]
        at += ref.shape[0]


def place_sums(where, mine, other, local):
    width = other.shape[1]
    return pl.pallas_call(
        place_sums_kernel,
        in_specs=[SMEM_WHOLE] + [VMEM_WHOLE] * 2,
        out_specs=[VMEM_WHOLE] * 3,
        out_shape=[sds((r, width), jnp.float32) for r in (3 * local, local, 24)],
        scratch_shapes=[pltpu.VMEM((2 * other.shape[0], width), jnp.float32)],
        compiler_params=params(),
        cost_estimate=cost(0, 6e6),
        name="place_sums",
    )(where, mine, other)


def in_back_kernel(where_ref, *refs):
    grads, (w_ref, x_ref, gh_ref, gain_ref, out_ref, sums_ref) = refs[:-6], refs[-6:]
    width = x_ref.shape[1]

    @pl.when(pl.program_id(0) == 0)
    def _():
        sums_ref[...] = jnp.zeros_like(sums_ref)

    @pl.when(pl.program_id(0) * BLOCK < where_ref[2])
    def _():
        e = 0.0
        for t in range(3):
            at = t * width
            for ref in grads[t::3]:
                e = e + mm(ref[...], w_ref[at : at + ref.shape[1], :])
                at += ref.shape[1]
        unit, inverse = norm_parts(x_ref[...].astype(jnp.float32))
        out_ref[...] = gh_ref[...] + norm_input_grad(e, unit, inverse, gain_ref[...])
        sums_ref[...] += column_sums(e * unit, e)


def in_back(where, shares, w, x, gh, gain):
    grads = [a for share in shares for a in share]
    width = x.shape[1]
    return pl.pallas_call(
        in_back_kernel,
        grid_spec=pltpu.PrefetchScalarGridSpec(
            num_scalar_prefetch=1,
            grid=(MOST // BLOCK,),
            in_specs=[live_block(a.shape[1]) for a in grads]
            + [fixed(w.shape), live_block(width), live_block(width), fixed(gain.shape)],
            out_specs=[live_block(width), fixed((8, width))],
        ),
        out_shape=[sds((TOTAL, width), jnp.float32), sds((8, width), jnp.float32)],
        compiler_params=params(),
        cost_estimate=cost(6 * 1024 * width * width, 20e6),
        name="in_back",
    )(where, *grads, w, x, gh, gain)


def unpack_kernel(info_ref, packed_ref, out_ref):
    slots = out_ref.shape[0]
    for seq in range(2):
        count = info_ref[seq]
        start = pl.multiple_of(info_ref[2 + seq], ROW_TILE)
        for at in range(0, slots, 128):
            size = min(128, slots - at)
            rows = packed_ref[pl.ds(pl.multiple_of(start + at, ROW_TILE), size), :]
            row_at = at + lax.broadcasted_iota(jnp.int32, rows.shape, 0)
            out_ref[pl.ds(at, size), seq, :] = jnp.where(row_at < count, rows, jnp.zeros_like(rows))


def unpack(info, packed, slots):
    width = packed.shape[1]
    out = pl.pallas_call(
        unpack_kernel,
        in_specs=[SMEM_WHOLE, VMEM_WHOLE],
        out_specs=VMEM_WHOLE,
        out_shape=sds((slots, 2, width), packed.dtype),
        compiler_params=params(),
        cost_estimate=cost(0, 10e6),
        name="unpack",
    )(info, packed)
    return out.transpose(1, 0, 2)


def shards(
    inputs,
    caption_lengths,
    g_attn,
    c_attn,
    w_qkv,
    b_qv,
    w_out,
    b_out,
    g_mlp,
    c_mlp,
    w_up,
    b_up,
    w_down,
    b_down,
    out_grad,
):
    seqs, slots, width = inputs.shape
    assert seqs == 2 and lax.axis_size("tensor") == 4 and lax.axis_size("dp") % PIECES == 0
    assert 2 * slots + ROW_TILE <= MOST
    local = w_qkv.shape[1]
    assert 4 * local == width and local <= 2 * PAIR
    place = lax.axis_index("dp")
    line_at = lax.axis_index("tensor")

    counts = jnp.minimum(caption_lengths + (IMAGE_ROWS + 1), slots)
    second_at = (counts[0] + (ROW_TILE - 1)) // ROW_TILE * ROW_TILE
    needed = second_at + counts[1]
    info = jnp.stack([counts[0], counts[1], jnp.int32(0), second_at, needed])
    where = jnp.stack([line_at, place & 1, needed, place & (PIECES - 1)])

    w_qkv_flat = w_qkv.reshape(3 * local, width)
    vec = jnp.concatenate([jnp.stack([b_out, g_mlp, c_mlp, b_down]), jnp.zeros((4, width), jnp.float32)])

    qkv_piece = own_piece(w_qkv_flat, b_qv.reshape(2 * local), place)
    units_piece = own_piece(jnp.concatenate([w_up, w_down]), b_up, place)
    x, normed_in = prepare(info, inputs, g_attn[None], c_attn[None])
    qkv_crossed = [across(d)(qkv_piece) for d in (1, 2, 3)]
    units_crossed = [across(d)(after(units_piece, normed_in)) for d in (1, 2, 3)]
    mine, theirs = gather_out(w_out, place)
    qkv_spread = [spread_plane(after(own, normed_in)) for own in qkv_crossed]
    g = pack(info, out_grad)
    qkv_quarters = [both_cores(four) for four in qkv_spread]
    own_bias = jnp.pad(b_qv.reshape(1, 2 * local), ((0, 0), (0, width - 2 * local)))
    w_qkv_all, bias = place_qkv(where, w_qkv_flat, own_bias, qkv_quarters)
    q, k, v = project(where, normed_in, w_qkv_all, bias)
    spread = [spread_plane(after(units_crossed[0], q))]
    mixture, stats = attend(info, q, k, v, unroll=3)
    spread += [spread_plane(after(own, mixture, g)) for own in units_crossed[1:]]
    quarters = [both_cores(spread[0], mixture)]
    w_out_all = place_out(where, mine, theirs)
    hidden, normed_mid = middle(where, x, mixture, w_out_all, vec)
    quarters.append(both_cores(spread[1], hidden))
    down, gmid, grad_w_down, grad_w_up, up_sums = own_units(where, normed_mid, g, w_up, b_up[None], w_down)
    quarters.append(both_cores(spread[2], down))
    grad_w_down, grad_w_up = lax.psum((grad_w_down, grad_w_up), "dp")
    down, gmid = other_units(where, quarters[0], normed_mid, g, down, gmid)
    down, gmid = other_units(where, quarters[1], normed_mid, g, down, gmid)
    out, gh, gmix, grad_w_out, mid_sums = last_units(
        where, quarters[2], normed_mid, g, down, gmid, hidden, mixture, vec, w_out_all, local
    )
    *own, qv_sums = attend_back(info, q, k, v, stats, gmix, 0, 2, 0)
    rest = own_grads(where, own, normed_in, grad_w_out, up_sums, mid_sums, qv_sums)
    kept, sent = core_halves(rest, place)
    got = exclusive(1)(sent)
    *some, _ = attend_back(info, q, k, v, stats, gmix, 2, 2, 2)
    outputs = unpack(info, out, slots)
    kept, got = plane_sums(kept + after(got, some[0]), place)
    stats = after(stats, grad_w_down, grad_w_up, outputs)
    *others, _ = attend_back(info, q, k, v, stats, gmix, 4, 2, 4)
    got = [after(a, others[0]) for a in got]
    got = spread_plane(whole_sum(kept + got[0] + got[1] + got[2]))
    back, in_sums = in_back(where, (own, some, others), w_qkv_all, x, gh, g_attn[None])
    rest = both_cores(got, in_sums)
    in_sums = whole_sum(in_sums + sum(exclusive(mask)(in_sums) for mask in (2, 4, 6)))
    in_sums = in_sums + exclusive(1)(in_sums)
    input_grad = unpack(info, back, slots)
    grad_w_qkv, grad_w_out, small = place_sums(where, *rest, local)
    up_sums, mid_sums, qv_sums = (small[8 * i : 8 * i + 8] for i in range(3))
    return (
        outputs,
        input_grad,
        in_sums[0],
        in_sums[1],
        grad_w_qkv.reshape(3, local, width),
        qv_sums[:2, :local],
        grad_w_out,
        mid_sums[2],
        mid_sums[0],
        mid_sums[1],
        grad_w_up,
        up_sums[0],
        grad_w_down,
        mid_sums[3],
    )


def solution(mesh):
    placed = (
        P("dp", None, None),
        P("dp"),
        P(),
        P(),
        P(None, "tensor", None),
        P(None, "tensor"),
        P("tensor", None),
        P(),
        P(),
        P(),
        P(None, "tensor"),
        P("tensor"),
        P("tensor", None),
        P(),
        P("dp", None, None),
    )
    return jax.shard_map(
        shards,
        mesh=mesh,
        in_specs=placed,
        out_specs=(
            P("dp", None, None),
            P("dp", None, None),
            P(),
            P(),
            P(None, "tensor", None),
            P(None, "tensor"),
            P("tensor", None),
            P(),
            P(),
            P(),
            P(None, "tensor"),
            P("tensor"),
            P("tensor", None),
            P(),
        ),
        check_vma=False,
    )
```

```python
import math
from functools import partial

import jax
import jax.numpy as jnp
from jax import lax
from jax.experimental import pallas as pl
from jax.experimental.pallas import tpu as pltpu
from jax.sharding import PartitionSpec as P

HEAD_DIM = 64
IMAGE_ROWS = 198
EPS = 1e-06
LOG2E = math.log2(math.e)
SCALE = HEAD_DIM ** (-0.5)
ROW_TILE = 16
QUERY_BLOCK = 256
BACK_BLOCK = 128
SLACK = 256
COST_SCALE = 0.02
VMEM_LIMIT = 48 * 1024 * 1024

NT = (((1,), (1,)), ((), ()))
TN = (((0,), (0,)), ((), ()))


def mm(a, b, dims=None):
    if dims is None:
        return jnp.dot(a, b, preferred_element_type=jnp.float32)
    return lax.dot_general(a, b, dims, preferred_element_type=jnp.float32)


def params():
    return pltpu.CompilerParams(vmem_limit_bytes=VMEM_LIMIT)


def cost(flops, moved, trans=0):
    scale = COST_SCALE
    return pl.CostEstimate(
        flops=int(flops * scale) + 1, bytes_accessed=int(moved * scale) + 1, transcendentals=int(trans * scale)
    )


def sds(shape, dtype):
    return jax.ShapeDtypeStruct(shape, dtype)


def after(value, *earlier):
    return lax.optimization_barrier((value,) + earlier)[0]


VMEM_WHOLE = pl.BlockSpec(memory_space=pltpu.VMEM)
SMEM_WHOLE = pl.BlockSpec(memory_space=pltpu.SMEM)


def norm_parts(values):
    average = jnp.mean(values, axis=-1, keepdims=True)
    centered = values - average
    squares = jnp.mean(centered * centered, axis=-1, keepdims=True)
    inverse = lax.rsqrt(squares + EPS)
    return centered * inverse, inverse


def norm_input_grad(grad_rows, unit_rows, inverse, gain):
    scaled = grad_rows * gain
    first = jnp.mean(scaled, axis=-1, keepdims=True)
    second = jnp.mean(scaled * unit_rows, axis=-1, keepdims=True)
    return inverse * (scaled - first - unit_rows * second)


def column_sums(*arrays):
    rows = [jnp.sum(a, axis=0, keepdims=True) for a in arrays]
    rows.append(jnp.zeros((8 - len(rows), rows[0].shape[1]), jnp.float32))
    return jnp.concatenate(rows, axis=0)


KEY_SIZES = (256, 384, 512, 640, 768)
PAIR = 2 * HEAD_DIM
STAT_BLOCKS = KEY_SIZES[-1] // QUERY_BLOCK


def key_size_cases(count, run):
    low = 0
    for size in KEY_SIZES:
        pl.when((count > low) & (count <= size))(partial(run, size))
        low = size


def split_heads(rows):
    first = lax.broadcasted_iota(jnp.int32, rows.shape, 1) < HEAD_DIM
    zero = jnp.zeros_like(rows)
    return jnp.concatenate([jnp.where(first, rows, zero), jnp.where(first, zero, rows)], axis=0)


def join_heads(both):
    kept = jnp.concatenate([both[:HEAD_DIM, :BACK_BLOCK], both[HEAD_DIM:, BACK_BLOCK:]], axis=0)
    return jnp.transpose(kept)


def pick_heads(both):
    first = lax.broadcasted_iota(jnp.int32, (QUERY_BLOCK, PAIR), 1) < HEAD_DIM
    return jnp.where(first, both[:QUERY_BLOCK], both[QUERY_BLOCK:])


def mask_tail(values, count, other):
    size = values.shape[0]
    tail = values[size - 128 :]
    key_at = (size - 128) + lax.broadcasted_iota(jnp.int32, tail.shape, 0)
    return jnp.concatenate([values[: size - 128], jnp.where(key_at < count, tail, other)], axis=0)


def attend_kernel(unroll, info_ref, q_ref, k_ref, v_ref, mixture_ref, stats_ref):
    pairs = q_ref.shape[1] // PAIR
    mixture_ref[...] = jnp.zeros_like(mixture_ref)

    for seq in range(2):
        count = info_ref[seq]
        start = pl.multiple_of(info_ref[2 + seq], ROW_TILE)

        def run(size, seq=seq, count=count, start=start):
            keys = pl.ds(start, size)

            def some_pairs(step, carry):
                lanes = [pl.ds(pl.multiple_of((step * unroll + u) * PAIR, PAIR), PAIR) for u in range(unroll)]

                def block(i, inner_carry):
                    rows = pl.ds(pl.multiple_of(start + i * QUERY_BLOCK, ROW_TILE), QUERY_BLOCK)
                    at = lax.broadcasted_iota(jnp.int32, (2 * QUERY_BLOCK, PAIR), 1)
                    stats = jnp.zeros((2 * QUERY_BLOCK, PAIR), jnp.float32)
                    for u in range(unroll):
                        q = split_heads(q_ref[rows, lanes[u]])
                        s = mm(q, k_ref[keys, lanes[u]], NT)
                        tail = s[:, size - 128 :]
                        key_at = (size - 128) + lax.broadcasted_iota(jnp.int32, tail.shape, 1)
                        tail = jnp.where(key_at < count, tail, -1e30)
                        s = jnp.concatenate([s[:, : size - 128], tail], axis=1)
                        top = jnp.max(s, axis=1, keepdims=True)
                        p = jnp.exp2((s - top) * (SCALE * LOG2E))
                        total = jnp.sum(p, axis=1, keepdims=True)
                        mixed = mm(p.astype(jnp.bfloat16), v_ref[keys, lanes[u]]) * (1.0 / total)
                        mixture_ref[rows, lanes[u]] = pick_heads(mixed).astype(jnp.bfloat16)
                        stats = jnp.where(at == u, top * (SCALE * LOG2E) + jnp.log2(total), stats)
                    stats = jnp.transpose(stats)
                    for u in range(unroll):
                        stats_ref[seq * STAT_BLOCKS + i, pl.ds(step * unroll + u, 1), :] = stats[u : u + 1, :]
                    return inner_carry

                lax.fori_loop(0, pl.cdiv(count, QUERY_BLOCK), block, 0)
                return carry

            lax.fori_loop(0, pairs // unroll, some_pairs, 0)

        key_size_cases(count, run)


def attend(info, q, k, v, unroll=2):
    total, width = q.shape
    return pl.pallas_call(
        partial(attend_kernel, unroll),
        in_specs=[SMEM_WHOLE] + [VMEM_WHOLE] * 3,
        out_specs=[VMEM_WHOLE] * 2,
        out_shape=[
            sds((total, width), jnp.bfloat16),
            sds((2 * STAT_BLOCKS, 8, 2 * QUERY_BLOCK), jnp.float32),
        ],
        compiler_params=params(),
        cost_estimate=cost(15e9, 2e7, 8e6),
        name="attend",
    )(info, q, k, v)


def attend_back_kernel(unroll, first, first_stat, info_ref, q_ref, k_ref, v_ref, stats_ref, g_ref, dq_ref, dk_ref, dv_ref, sums_ref, turned_ref, ak_ref, av_ref):
    pairs = dq_ref.shape[1] // PAIR
    sums_ref[...] = jnp.zeros_like(sums_ref)
    dq_ref[...] = jnp.zeros_like(dq_ref)
    dk_ref[...] = jnp.zeros_like(dk_ref)
    dv_ref[...] = jnp.zeros_like(dv_ref)

    for seq in range(2):
        count = info_ref[seq]
        start = pl.multiple_of(info_ref[2 + seq], ROW_TILE)

        def run(size, seq=seq, count=count, start=start):
            keys = pl.ds(start, size)
            here = pl.ds(0, size)

            def some_pairs(step, carry):
                lanes = [pl.ds(pl.multiple_of((first + step * unroll + u) * PAIR, PAIR), PAIR) for u in range(unroll)]
                to = [pl.ds(pl.multiple_of((step * unroll + u) * PAIR, PAIR), PAIR) for u in range(unroll)]
                for u in range(unroll):
                    turned_ref[u, :, here] = jnp.transpose(k_ref[keys, lanes[u]])
                    ak_ref[u, here, :] = jnp.zeros((size, PAIR), jnp.float32)
                    av_ref[u, here, :] = jnp.zeros((size, PAIR), jnp.float32)

                def block(i, inner_carry):
                    row = pl.multiple_of(start + i * BACK_BLOCK, ROW_TILE)
                    rows = pl.ds(row, BACK_BLOCK)
                    row_at = lax.broadcasted_iota(jnp.int32, (BACK_BLOCK, PAIR), 0)
                    live = row_at < count - i * BACK_BLOCK
                    for u in range(unroll):
                        q = split_heads(q_ref[rows, lanes[u]])
                        g = g_ref[rows, lanes[u]]
                        g = split_heads(jnp.where(live, g, jnp.zeros_like(g)))
                        half = pl.multiple_of((i & 1) * BACK_BLOCK, BACK_BLOCK)
                        at = (seq * STAT_BLOCKS + (i >> 1), pl.ds(first_stat + step * unroll + u, 1))
                        stats = [stats_ref[(*at, pl.ds(h + half, BACK_BLOCK))] for h in (0, QUERY_BLOCK)]
                        stats = jnp.concatenate(stats, axis=1)
                        s = mm(k_ref[keys, lanes[u]], q, NT) * (SCALE * LOG2E) - stats
                        w = jnp.exp2(mask_tail(s, count, -1e30))
                        dw = mm(v_ref[keys, lanes[u]], g, NT)
                        av_ref[u, here, :] += mm(w.astype(jnp.bfloat16), g)
                        inner = jnp.sum(w * dw, axis=0, keepdims=True)
                        ds = (w * (dw - inner)).astype(jnp.bfloat16)
                        ak_ref[u, here, :] += mm(ds, q)
                        dq = join_heads(mm(turned_ref[u, :, here], ds)) * SCALE
                        dq_ref[rows, to[u]] = dq.astype(jnp.bfloat16)
                        sums_ref[0:1, to[u]] += jnp.sum(dq, axis=0, keepdims=True)
                    return inner_carry

                lax.fori_loop(0, pl.cdiv(count, BACK_BLOCK), block, 0)
                for u in range(unroll):
                    dk_ref[keys, to[u]] = (ak_ref[u, here, :] * SCALE).astype(jnp.bfloat16)
                    dv = av_ref[u, here, :]
                    dv_ref[keys, to[u]] = dv.astype(jnp.bfloat16)
                    sums_ref[1:2, to[u]] += jnp.sum(dv, axis=0, keepdims=True)
                return carry

            lax.fori_loop(0, pairs // unroll, some_pairs, 0)

        key_size_cases(count, run)


def attend_back(info, q, k, v, stats, g, first, pairs, first_stat, unroll=2):
    total = q.shape[0]
    width = pairs * PAIR
    return pl.pallas_call(
        partial(attend_back_kernel, unroll, first, first_stat),
        in_specs=[SMEM_WHOLE] + [VMEM_WHOLE] * 5,
        out_specs=[VMEM_WHOLE] * 4,
        out_shape=[sds((total, width), jnp.bfloat16)] * 3 + [sds((8, width), jnp.float32)],
        scratch_shapes=[
            pltpu.VMEM((unroll, PAIR, KEY_SIZES[-1]), jnp.bfloat16),
            pltpu.VMEM((unroll, KEY_SIZES[-1], PAIR), jnp.float32),
            pltpu.VMEM((unroll, KEY_SIZES[-1], PAIR), jnp.float32),
        ],
        compiler_params=params(),
        cost_estimate=cost(5e9 * pairs, 2e7, 1e6 * pairs),
        name="attend_back",
    )(info, q, k, v, stats, g)

BLOCK = 256
CHUNK = 128
MOST = 1536
TOTAL = MOST + SLACK


def pack_rows(info_ref, pair_ref, out_ref):
    slots = pair_ref.shape[1]
    out_ref[...] = jnp.zeros_like(out_ref)
    for seq in range(2):
        count = info_ref[seq]
        start = pl.multiple_of(info_ref[2 + seq], ROW_TILE)
        for at in range(0, slots, 128):
            size = min(128, slots - at)

            @pl.when(count > at)
            def _(seq=seq, at=at, size=size, count=count, start=start):
                rows = pair_ref[seq, pl.ds(at, size), :]
                row_at = at + lax.broadcasted_iota(jnp.int32, rows.shape, 0)
                rows = jnp.where(row_at < count, rows, jnp.bfloat16(0))
                out_ref[pl.ds(pl.multiple_of(start + at, ROW_TILE), size), :] = rows


def prepare_kernel(info_ref, pair_ref, gain_ref, shift_ref, x_ref, normed_ref):
    pack_rows(info_ref, pair_ref, x_ref)
    needed = info_ref[4]
    for at in range(0, TOTAL, 128):
        here = pl.ds(at, 128)

        @pl.when(at < needed)
        def _(here=here):
            unit, _ = norm_parts(x_ref[here, :].astype(jnp.float32))
            normed_ref[here, :] = (unit * gain_ref[...] + shift_ref[...]).astype(jnp.bfloat16)

        @pl.when(at >= needed)
        def _(here=here):
            normed_ref[here, :] = jnp.zeros((128, normed_ref.shape[1]), jnp.bfloat16)


def prepare(info, pair, gain, shift):
    width = pair.shape[2]
    return pl.pallas_call(
        prepare_kernel,
        in_specs=[SMEM_WHOLE] + [VMEM_WHOLE] * 3,
        out_specs=[VMEM_WHOLE] * 2,
        out_shape=[sds((TOTAL, width), jnp.bfloat16)] * 2,
        compiler_params=params(),
        cost_estimate=cost(0, 9e6),
        name="prepare",
    )(info, pair, gain, shift)


def pack(info, pair):
    return pl.pallas_call(
        pack_rows,
        in_specs=[SMEM_WHOLE, VMEM_WHOLE],
        out_specs=VMEM_WHOLE,
        out_shape=sds((MOST, pair.shape[2]), pair.dtype),
        compiler_params=params(),
        cost_estimate=cost(0, 5e6),
        name="pack",
    )(info, pair)


PIECES = 8


def exclusive(mask):
    return lambda value: lax.ppermute(
        value, "dp", [(i, i ^ mask) for i in range(lax.axis_size("dp"))]
    )


def across(mask):
    return lambda value: lax.ppermute(value, "tensor", [(i, i ^ mask) for i in range(4)])


def own_piece(rows, extra, place):
    count = rows.shape[0] // PIECES
    mine = lax.dynamic_slice_in_dim(rows, (place & (PIECES - 1)) * count, count).astype(jnp.float32)
    extra = jnp.pad(extra[None], ((0, 7), (0, rows.shape[1] - extra.shape[0])))
    return jnp.concatenate([mine, extra])


def spread_plane(own):
    return [own] + [exclusive(mask)(own) for mask in (2, 4, 6)]


def both_cores(four, *earlier):
    mine = jnp.concatenate([after(four[0], *earlier)] + four[1:] if earlier else four)
    return mine, exclusive(1)(mine)


def gather_out(w_out, place):
    half = w_out.shape[0] // 2
    mine = lax.dynamic_slice_in_dim(w_out, (place & 1) * half, half).astype(jnp.float32)
    mine = lax.all_gather(mine, "tensor")
    return mine, exclusive(1)(mine)


def place_pieces(place, mine_ref, other_ref, extra, to_ref, cast):
    rows = other_ref.shape[0] // 4 - extra
    for at in range(4):
        for core, ref in enumerate((mine_ref, other_ref)):
            to = pl.multiple_of((place ^ (2 * at + core)) * rows, 8)
            to_ref[pl.ds(to, rows), :] = cast(ref[at * (rows + extra) : at * (rows + extra) + rows, :])


def place_qkv_kernel(where_ref, own_ref, own_bias_ref, *rest):
    quarters, (w_ref, bias_ref, flat_ref) = rest[:6], rest[6:]
    width = w_ref.shape[1]
    local = own_ref.shape[0] // 3
    bias_ref[...] = jnp.zeros_like(bias_ref)
    for at in range(4):
        if at:
            mine, other = quarters[2 * at - 2 : 2 * at]
            place_pieces(where_ref[3], mine, other, 8, flat_ref, lambda piece: piece)
            rows = mine.shape[0] // 4 - 8
            biases = mine[rows : rows + 1, :]
        else:
            biases = own_bias_ref[...]
        for t in range(3):
            part = (flat_ref if at else own_ref)[t * local : (t + 1) * local, :]
            w_ref[t * width + at * local : t * width + (at + 1) * local, :] = part.astype(jnp.bfloat16)
        bias_ref[0:1, at * local : (at + 1) * local] = biases[:, 0:local]
        bias_ref[0:1, 2 * width + at * local : 2 * width + (at + 1) * local] = biases[:, local : 2 * local]


def place_qkv(where, own, own_bias, quarters):
    operands = [where, own, own_bias]
    for quarter in quarters:
        operands += quarter
    wide, width = own.shape
    return pl.pallas_call(
        place_qkv_kernel,
        in_specs=[SMEM_WHOLE] + [VMEM_WHOLE] * (len(operands) - 1),
        out_specs=[VMEM_WHOLE] * 2,
        out_shape=[sds((4 * wide, width), jnp.bfloat16), sds((8, 4 * wide), jnp.float32)],
        scratch_shapes=[pltpu.VMEM((wide, width), jnp.float32)],
        compiler_params=params(),
        cost_estimate=cost(0, 12e6),
        name="place_qkv",
    )(*operands)


def place_out_kernel(where_ref, mine_ref, theirs_ref, w_ref):
    half = mine_ref.shape[1]
    for at in range(4):
        for core in range(2):
            to = pl.multiple_of(at * 2 * half + (where_ref[1] ^ core) * half, ROW_TILE)
            from_ref = (mine_ref, theirs_ref)[core]
            w_ref[pl.ds(to, half), :] = from_ref[where_ref[0] ^ at].astype(jnp.bfloat16)


def place_out(where, mine, theirs):
    width = mine.shape[2]
    return pl.pallas_call(
        place_out_kernel,
        in_specs=[SMEM_WHOLE, VMEM_WHOLE, VMEM_WHOLE],
        out_specs=VMEM_WHOLE,
        out_shape=sds((8 * mine.shape[1], width), jnp.bfloat16),
        compiler_params=params(),
        cost_estimate=cost(0, 4e6),
        name="place_out",
    )(where, mine, theirs)


def live_block(width):
    return pl.BlockSpec((BLOCK, width), lambda i, where: (jnp.minimum(i, (where[2] - 1) // BLOCK), 0))


def every_block(width):
    return pl.BlockSpec((BLOCK, width), lambda i, where: (i, 0))


def fixed(shape):
    return pl.BlockSpec(shape, lambda i, where: (0,) * len(shape))


def project_kernel(where_ref, normed_ref, w_ref, bias_ref, *outs):
    width = normed_ref.shape[1]

    @pl.when(pl.program_id(0) * BLOCK < where_ref[2])
    def _():
        for t, out in enumerate(outs):
            here = slice(t * width, (t + 1) * width)
            out[...] = (mm(normed_ref[...], w_ref[here, :], NT) + bias_ref[0:1, here]).astype(jnp.bfloat16)

    @pl.when(pl.program_id(0) * BLOCK >= where_ref[2])
    def _():
        for out in outs:
            out[...] = jnp.zeros_like(out)


def project(where, normed, w, bias):
    width = normed.shape[1]
    return pl.pallas_call(
        project_kernel,
        grid_spec=pltpu.PrefetchScalarGridSpec(
            num_scalar_prefetch=1,
            grid=(TOTAL // BLOCK,),
            in_specs=[live_block(width), fixed(w.shape), fixed(bias.shape)],
            out_specs=[every_block(width)] * 3,
        ),
        out_shape=[sds((TOTAL, width), jnp.bfloat16)] * 3,
        compiler_params=params(),
        cost_estimate=cost(2 * 1024 * width * w.shape[0], 15e6),
        name="project",
    )(where, normed, w, bias)


def middle_kernel(where_ref, x_ref, mixture_ref, w_ref, vec_ref, hidden_ref, normed_ref):
    @pl.when(pl.program_id(0) * BLOCK < where_ref[2])
    def _():
        hidden = x_ref[...].astype(jnp.float32) + mm(mixture_ref[...], w_ref[...]) + vec_ref[0:1, :]
        row_at = pl.program_id(0) * BLOCK + lax.broadcasted_iota(jnp.int32, hidden.shape, 0)
        hidden = jnp.where(row_at < where_ref[2], hidden, 0.0)
        hidden_ref[...] = hidden
        unit, _ = norm_parts(hidden)
        normed_ref[...] = (unit * vec_ref[1:2, :] + vec_ref[2:3, :]).astype(jnp.bfloat16)


def middle(where, x, mixture, w, vec):
    width = x.shape[1]
    return pl.pallas_call(
        middle_kernel,
        grid_spec=pltpu.PrefetchScalarGridSpec(
            num_scalar_prefetch=1,
            grid=(MOST // BLOCK,),
            in_specs=[live_block(width), live_block(width), fixed(w.shape), fixed(vec.shape)],
            out_specs=[live_block(width)] * 2,
        ),
        out_shape=[sds((MOST, width), jnp.float32), sds((MOST, width), jnp.bfloat16)],
        compiler_params=params(),
        cost_estimate=cost(2 * 1024 * width * width, 1024 * width * 10),
        name="middle",
    )(where, x, mixture, w, vec)


def feed_forward(normed, g, w_up, b_up, w_down):
    up = mm(normed, w_up) + b_up
    cdf = 0.5 + 0.5 * lax.erf(up * (0.5**0.5))
    act = (up * cdf).astype(jnp.bfloat16)
    slope = cdf + up * (jnp.exp(-0.5 * up * up) * (1.0 / math.sqrt(2.0 * math.pi)))
    gup = mm(g, w_down, NT) * slope
    gul = gup.astype(jnp.bfloat16)
    return act, gup, gul, mm(act, w_down), mm(gul, w_up, NT)


def own_units_kernel(where_ref, normed_ref, g_ref, w_up_ref, b_up_ref, w_down_ref, *rest):
    down_ref, gmid_ref, grad_down_ref, grad_up_ref, sums_ref = rest

    @pl.when(pl.program_id(0) == 0)
    def _():
        grad_down_ref[...] = jnp.zeros_like(grad_down_ref)
        grad_up_ref[...] = jnp.zeros_like(grad_up_ref)
        sums_ref[...] = jnp.zeros_like(sums_ref)

    @pl.when(pl.program_id(0) * BLOCK < where_ref[2])
    def _():
        normed, g = normed_ref[...], g_ref[...]
        act, gup, gul, down, gmid = feed_forward(normed, g, w_up_ref[...], b_up_ref[...], w_down_ref[...])
        down_ref[...] = down
        gmid_ref[...] = gmid
        grad_down_ref[...] += mm(act, g, TN)
        grad_up_ref[...] += mm(normed, gul, TN)
        sums_ref[...] += column_sums(gup)


def own_units(where, normed, g, w_up, b_up, w_down):
    width, units = w_up.shape
    return pl.pallas_call(
        own_units_kernel,
        grid_spec=pltpu.PrefetchScalarGridSpec(
            num_scalar_prefetch=1,
            grid=(MOST // BLOCK,),
            in_specs=[
                live_block(width),
                live_block(width),
                fixed(w_up.shape),
                fixed(b_up.shape),
                fixed(w_down.shape),
            ],
            out_specs=[
                live_block(width),
                live_block(width),
                fixed((units, width)),
                fixed((width, units)),
                fixed((8, units)),
            ],
        ),
        out_shape=[
            sds((MOST, width), jnp.float32),
            sds((MOST, width), jnp.float32),
            sds((units, width), jnp.float32),
            sds((width, units), jnp.float32),
            sds((8, units), jnp.float32),
        ],
        compiler_params=params(),
        cost_estimate=cost(12 * 1024 * width * units, 25e6, 3e6),
        name="own_units",
    )(where, normed, g, w_up, b_up, w_down)


def place_weights(where_ref, mine_ref, other_ref, w_ref, b_ref):
    place_pieces(where_ref[3], mine_ref, other_ref, 8, w_ref, lambda piece: piece.astype(jnp.bfloat16))
    rows = mine_ref.shape[0] // 4 - 8
    b_ref[...] = mine_ref[rows : rows + 8, :]


def other_units_kernel(where_ref, mine_ref, other_ref, normed_ref, g_ref, *rest):
    down_in_ref, gmid_in_ref, down_ref, gmid_ref, w_ref, b_ref = rest
    width = normed_ref.shape[1]

    @pl.when(pl.program_id(0) == 0)
    def _():
        place_weights(where_ref, mine_ref, other_ref, w_ref, b_ref)

    @pl.when(pl.program_id(0) * BLOCK < where_ref[2])
    def _():
        _, _, _, down, gmid = feed_forward(
            normed_ref[...], g_ref[...], w_ref[0:width, :], b_ref[0:1, :], w_ref[width:, :]
        )
        down_ref[...] = down_in_ref[...] + down
        gmid_ref[...] = gmid_in_ref[...] + gmid


def other_units(where, quarter, normed, g, down, gmid):
    mine, other = quarter
    width = normed.shape[1]
    units = other.shape[1]
    return pl.pallas_call(
        other_units_kernel,
        grid_spec=pltpu.PrefetchScalarGridSpec(
            num_scalar_prefetch=1,
            grid=(MOST // BLOCK,),
            in_specs=[fixed(mine.shape), fixed(other.shape)] + [live_block(width)] * 4,
            out_specs=[live_block(width)] * 2,
            scratch_shapes=[pltpu.VMEM((2 * width, units), jnp.bfloat16), pltpu.VMEM((8, units), jnp.float32)],
        ),
        out_shape=[sds((MOST, width), jnp.float32)] * 2,
        input_output_aliases={5: 0, 6: 1},
        compiler_params=params(),
        cost_estimate=cost(8 * 1024 * width * units, 25e6, 3e6),
        name="other_units",
    )(where, mine, other, normed, g, down, gmid)


def last_units_kernel(where_ref, mine_ref, other_ref, normed_ref, g_ref, *rest):
    (down_in_ref, gmid_in_ref, hidden_ref, mixture_ref, vec_ref, w_out_ref) = rest[:6]
    (out_ref, gh_ref, gmix_ref, grad_w_out_ref, sums_ref, w_ref, b_ref) = rest[6:]
    width = normed_ref.shape[1]

    @pl.when(pl.program_id(0) == 0)
    def _():
        place_weights(where_ref, mine_ref, other_ref, w_ref, b_ref)
        grad_w_out_ref[...] = jnp.zeros_like(grad_w_out_ref)
        sums_ref[...] = jnp.zeros_like(sums_ref)

    @pl.when(pl.program_id(0) * BLOCK < where_ref[2])
    def _():
        g = g_ref[...]
        _, _, _, down, gmid = feed_forward(normed_ref[...], g, w_ref[0:width, :], b_ref[0:1, :], w_ref[width:, :])
        hidden = hidden_ref[...]
        out_ref[...] = (hidden + (down_in_ref[...] + down) + vec_ref[3:4, :]).astype(jnp.bfloat16)
        e = gmid_in_ref[...] + gmid
        unit, inverse = norm_parts(hidden)
        g = g.astype(jnp.float32)
        gh = g + norm_input_grad(e, unit, inverse, vec_ref[1:2, :])
        gh_ref[...] = gh
        ghl = gh.astype(jnp.bfloat16)
        gmix_ref[...] = mm(ghl, w_out_ref[...], NT).astype(jnp.bfloat16)
        grad_w_out_ref[...] += mm(mixture_ref[...], ghl, TN)[0 : grad_w_out_ref.shape[0], :]
        sums_ref[...] += column_sums(e * unit, e, gh, g)


def last_units(where, quarter, normed, g, down, gmid, hidden, mixture, vec, w_out, local):
    mine, other = quarter
    width = normed.shape[1]
    units = other.shape[1]
    return pl.pallas_call(
        last_units_kernel,
        grid_spec=pltpu.PrefetchScalarGridSpec(
            num_scalar_prefetch=1,
            grid=(MOST // BLOCK,),
            in_specs=[fixed(mine.shape), fixed(other.shape)]
            + [live_block(width)] * 5
            + [pl.BlockSpec((BLOCK, 2 * PAIR), lambda i, where: (jnp.minimum(i, (where[2] - 1) // BLOCK), 0))]
            + [fixed(vec.shape), fixed(w_out.shape)],
            out_specs=[
                live_block(width),
                live_block(width),
                live_block(width),
                fixed((local, width)),
                fixed((8, width)),
            ],
            scratch_shapes=[pltpu.VMEM((2 * width, units), jnp.bfloat16), pltpu.VMEM((8, units), jnp.float32)],
        ),
        out_shape=[
            sds((MOST, width), jnp.bfloat16),
            sds((MOST, width), jnp.float32),
            sds((TOTAL, width), jnp.bfloat16),
            sds((local, width), jnp.float32),
            sds((8, width), jnp.float32),
        ],
        compiler_params=params(),
        cost_estimate=cost(10 * 1024 * width * units, 35e6, 3e6),
        name="last_units",
    )(where, mine, other, normed, g, down, gmid, hidden, mixture, vec, w_out)


def own_grads_kernel(where_ref, dq_ref, dk_ref, dv_ref, normed_ref, *rest):
    grad_out_ref, up_ref, mid_ref, qv_ref, all_ref = rest
    local, width = grad_out_ref.shape

    @pl.when(pl.program_id(0) == 0)
    def _():
        all_ref[...] = jnp.zeros_like(all_ref)
        at = 3 * local
        for ref in (grad_out_ref, up_ref, mid_ref, qv_ref):
            all_ref[at : at + ref.shape[0], 0 : ref.shape[1]] = ref[...]
            at += ref.shape[0]

    @pl.when(pl.program_id(0) * BLOCK < where_ref[2])
    def _():
        for t, ref in enumerate((dq_ref, dk_ref, dv_ref)):
            here = slice(t * local, (t + 1) * local)
            all_ref[here, :] += mm(ref[...], normed_ref[...], TN)[0:local, :]


def own_grads(where, three, normed, *whole):
    local, width = whole[0].shape
    rows = 3 * local + sum(a.shape[0] for a in whole)
    rows = -(-rows // (8 * PIECES)) * 8 * PIECES
    return pl.pallas_call(
        own_grads_kernel,
        grid_spec=pltpu.PrefetchScalarGridSpec(
            num_scalar_prefetch=1,
            grid=(MOST // BLOCK,),
            in_specs=[live_block(a.shape[1]) for a in three]
            + [live_block(width)]
            + [fixed(a.shape) for a in whole],
            out_specs=fixed((rows, width)),
        ),
        out_shape=sds((rows, width), jnp.float32),
        compiler_params=params(),
        cost_estimate=cost(6 * 1024 * width * local, 12e6),
        name="own_grads",
    )(where, *three, normed, *whole)


def core_halves(rows, place):
    pieces = rows.reshape(4, 2, rows.shape[0] // PIECES, rows.shape[1])
    return [
        lax.dynamic_index_in_dim(pieces, core, 1, keepdims=False) for core in (place & 1, 1 - (place & 1))
    ]


def plane_sums(half, place):
    plane = (place >> 1) & 3
    pick = lambda at: lax.dynamic_index_in_dim(half, plane ^ at, 0, keepdims=False)
    return pick(0), [exclusive(2 * at)(pick(at)) for at in (1, 2, 3)]


def whole_sum(total):
    size = lax.axis_size("dp")
    if size > PIECES:
        groups = [list(range(i, size, PIECES)) for i in range(PIECES)]
        total = lax.psum(total, "dp", axis_index_groups=groups)
    return total


def place_sums_kernel(where_ref, mine_ref, other_ref, qkv_ref, out_ref, small_ref, all_ref):
    place_pieces(where_ref[3], mine_ref, other_ref, 0, all_ref, lambda piece: piece)
    at = 0
    for ref in (qkv_ref, out_ref, small_ref):
        ref[...] = all_ref[at : at + ref.shape[0], :]
        at += ref.shape[0]


def place_sums(where, mine, other, local):
    width = other.shape[1]
    return pl.pallas_call(
        place_sums_kernel,
        in_specs=[SMEM_WHOLE] + [VMEM_WHOLE] * 2,
        out_specs=[VMEM_WHOLE] * 3,
        out_shape=[sds((r, width), jnp.float32) for r in (3 * local, local, 24)],
        scratch_shapes=[pltpu.VMEM((2 * other.shape[0], width), jnp.float32)],
        compiler_params=params(),
        cost_estimate=cost(0, 6e6),
        name="place_sums",
    )(where, mine, other)


def in_back_kernel(where_ref, info_ref, *refs):
    grads, (w_ref, x_ref, gh_ref, gain_ref, out_ref, sums_ref, packed_ref) = refs[:-7], refs[-7:]
    width = x_ref.shape[1]

    @pl.when(pl.program_id(0) == 0)
    def _():
        sums_ref[...] = jnp.zeros_like(sums_ref)

    @pl.when(pl.program_id(0) * BLOCK < where_ref[2])
    def _():
        e = 0.0
        for t in range(3):
            at = t * width
            for ref in grads[t::3]:
                e = e + mm(ref[...], w_ref[at : at + ref.shape[1], :])
                at += ref.shape[1]
        unit, inverse = norm_parts(x_ref[...].astype(jnp.float32))
        here = pl.ds(pl.multiple_of(pl.program_id(0) * BLOCK, BLOCK), BLOCK)
        packed_ref[here, :] = gh_ref[...] + norm_input_grad(e, unit, inverse, gain_ref[...])
        sums_ref[...] += column_sums(e * unit, e)

    @pl.when(pl.program_id(0) == pl.num_programs(0) - 1)
    def _():
        unpack_kernel(info_ref, packed_ref, out_ref)


def in_back(where, info, shares, w, x, gh, gain, slots):
    grads = [a for share in shares for a in share]
    width = x.shape[1]
    back, sums = pl.pallas_call(
        in_back_kernel,
        grid_spec=pltpu.PrefetchScalarGridSpec(
            num_scalar_prefetch=1,
            grid=(MOST // BLOCK,),
            in_specs=[SMEM_WHOLE]
            + [live_block(a.shape[1]) for a in grads]
            + [fixed(w.shape), live_block(width), live_block(width), fixed(gain.shape)],
            out_specs=[fixed((slots, 2, width)), fixed((8, width))],
            scratch_shapes=[pltpu.VMEM((MOST, width), jnp.float32)],
        ),
        out_shape=[sds((slots, 2, width), jnp.float32), sds((8, width), jnp.float32)],
        compiler_params=params(),
        cost_estimate=cost(6 * 1024 * width * width, 20e6),
        name="in_back",
    )(where, info, *grads, w, x, gh, gain)
    return back.transpose(1, 0, 2), sums


def unpack_kernel(info_ref, packed_ref, out_ref):
    slots = out_ref.shape[0]
    for seq in range(2):
        count = info_ref[seq]
        start = pl.multiple_of(info_ref[2 + seq], ROW_TILE)
        for at in range(0, slots, 128):
            size = min(128, slots - at)
            rows = packed_ref[pl.ds(pl.multiple_of(start + at, ROW_TILE), size), :]
            row_at = at + lax.broadcasted_iota(jnp.int32, rows.shape, 0)
            out_ref[pl.ds(at, size), seq, :] = jnp.where(row_at < count, rows, jnp.zeros_like(rows))


def unpack(info, packed, slots):
    width = packed.shape[1]
    out = pl.pallas_call(
        unpack_kernel,
        in_specs=[SMEM_WHOLE, VMEM_WHOLE],
        out_specs=VMEM_WHOLE,
        out_shape=sds((slots, 2, width), packed.dtype),
        compiler_params=params(),
        cost_estimate=cost(0, 10e6),
        name="unpack",
    )(info, packed)
    return out.transpose(1, 0, 2)


def shards(
    inputs,
    caption_lengths,
    g_attn,
    c_attn,
    w_qkv,
    b_qv,
    w_out,
    b_out,
    g_mlp,
    c_mlp,
    w_up,
    b_up,
    w_down,
    b_down,
    out_grad,
):
    seqs, slots, width = inputs.shape
    assert seqs == 2 and lax.axis_size("tensor") == 4 and lax.axis_size("dp") % PIECES == 0
    assert 2 * slots + ROW_TILE <= MOST
    local = w_qkv.shape[1]
    assert 4 * local == width and local <= 2 * PAIR
    place = lax.axis_index("dp")
    line_at = lax.axis_index("tensor")

    counts = jnp.minimum(caption_lengths + (IMAGE_ROWS + 1), slots)
    second_at = (counts[0] + (ROW_TILE - 1)) // ROW_TILE * ROW_TILE
    needed = second_at + counts[1]
    info = jnp.stack([counts[0], counts[1], jnp.int32(0), second_at, needed])
    where = jnp.stack([line_at, place & 1, needed, place & (PIECES - 1)])

    w_qkv_flat = w_qkv.reshape(3 * local, width)
    vec = jnp.concatenate([jnp.stack([b_out, g_mlp, c_mlp, b_down]), jnp.zeros((4, width), jnp.float32)])

    qkv_piece = own_piece(w_qkv_flat, b_qv.reshape(2 * local), place)
    units_piece = own_piece(jnp.concatenate([w_up, w_down]), b_up, place)
    x, normed_in = prepare(info, inputs, g_attn[None], c_attn[None])
    qkv_crossed = [across(d)(qkv_piece) for d in (1, 2, 3)]
    units_crossed = [across(d)(after(units_piece, normed_in)) for d in (1, 2, 3)]
    mine, theirs = gather_out(w_out, place)
    qkv_spread = [spread_plane(after(own, normed_in)) for own in qkv_crossed]
    g = pack(info, out_grad)
    qkv_quarters = [both_cores(four) for four in qkv_spread]
    own_bias = jnp.pad(b_qv.reshape(1, 2 * local), ((0, 0), (0, width - 2 * local)))
    w_qkv_all, bias = place_qkv(where, w_qkv_flat, own_bias, qkv_quarters)
    q, k, v = project(where, normed_in, w_qkv_all, bias)
    spread = [spread_plane(after(units_crossed[0], q))]
    mixture, stats = attend(info, q, k, v, unroll=3)
    spread += [spread_plane(after(own, mixture, g)) for own in units_crossed[1:]]
    quarters = [both_cores(spread[0], mixture)]
    w_out_all = place_out(where, mine, theirs)
    hidden, normed_mid = middle(where, x, mixture, w_out_all, vec)
    quarters.append(both_cores(spread[1], hidden))
    down, gmid, grad_w_down, grad_w_up, up_sums = own_units(where, normed_mid, g, w_up, b_up[None], w_down)
    quarters.append(both_cores(spread[2], down))
    grad_w_down, grad_w_up = lax.psum((grad_w_down, grad_w_up), "dp")
    down, gmid = other_units(where, quarters[0], normed_mid, g, down, gmid)
    down, gmid = other_units(where, quarters[1], normed_mid, g, down, gmid)
    out, gh, gmix, grad_w_out, mid_sums = last_units(
        where, quarters[2], normed_mid, g, down, gmid, hidden, mixture, vec, w_out_all, local
    )
    *own, qv_sums = attend_back(info, q, k, v, stats, gmix, 0, 2, 0)
    rest = own_grads(where, own, normed_in, grad_w_out, up_sums, mid_sums, qv_sums)
    kept, sent = core_halves(rest, place)
    got = exclusive(1)(sent)
    *some, _ = attend_back(info, q, k, v, stats, gmix, 2, 2, 2)
    outputs = unpack(info, out, slots)
    kept, got = plane_sums(kept + after(got, some[0]), place)
    stats = after(stats, grad_w_down, grad_w_up, outputs)
    *others, _ = attend_back(info, q, k, v, stats, gmix, 4, 2, 4)
    got = [after(a, others[0]) for a in got]
    got = spread_plane(whole_sum(kept + got[0] + got[1] + got[2]))
    input_grad, in_sums = in_back(where, info, (own, some, others), w_qkv_all, x, gh, g_attn[None], slots)
    rest = both_cores(got, in_sums)
    in_sums = whole_sum(in_sums + sum(exclusive(mask)(in_sums) for mask in (2, 4, 6)))
    in_sums = in_sums + exclusive(1)(in_sums)
    grad_w_qkv, grad_w_out, small = place_sums(where, *rest, local)
    up_sums, mid_sums, qv_sums = (small[8 * i : 8 * i + 8] for i in range(3))
    return (
        outputs,
        input_grad,
        in_sums[0],
        in_sums[1],
        grad_w_qkv.reshape(3, local, width),
        qv_sums[:2, :local],
        grad_w_out,
        mid_sums[2],
        mid_sums[0],
        mid_sums[1],
        grad_w_up,
        up_sums[0],
        grad_w_down,
        mid_sums[3],
    )


def solution(mesh):
    placed = (
        P("dp", None, None),
        P("dp"),
        P(),
        P(),
        P(None, "tensor", None),
        P(None, "tensor"),
        P("tensor", None),
        P(),
        P(),
        P(),
        P(None, "tensor"),
        P("tensor"),
        P("tensor", None),
        P(),
        P("dp", None, None),
    )
    return jax.shard_map(
        shards,
        mesh=mesh,
        in_specs=placed,
        out_specs=(
            P("dp", None, None),
            P("dp", None, None),
            P(),
            P(),
            P(None, "tensor", None),
            P(None, "tensor"),
            P("tensor", None),
            P(),
            P(),
            P(),
            P(None, "tensor"),
            P("tensor"),
            P("tensor", None),
            P(),
        ),
        check_vma=False,
    )
```
